256 devices in a mesh: axial: 16 (over z, core), depth: 16 (over x, y).
Axes of the slice: x: 4, y: 4, z: 8, core: 2. Of those that a mesh axis runs over, the one named last changes fastest.
Arguments:
- kelvin_before_step: float32 [256, 128, 2048], P('axial', 'depth'), may hold values from -3 to 3
- unburnt_resin_share: float32 [256, 128, 2048], P('axial', 'depth'), may hold values from 0.2 to 1
- deposited_energy_amount: float32 [256, 128, 2048], P('axial', 'depth'), may hold values from -6 to 6
- material_label: int32 [256, 128, 2048], P('axial', 'depth'), may hold values from 0 to 7
- zonal_diffusivity: float32 [8], replicated, may hold values from 0.5 to 2
- zonal_storage_coefficient: float32 [8], replicated, may hold values from 0.05 to 0.5
- frequency_coefficient: float32 [8], replicated, may hold values from 0.2 to 2
- arrhenius_barrier: float32 [8], replicated, may hold values from 1 to 4
- stream_keeper: int32 [256, 2048], P('axial', 'depth'), may hold values from 0 to 15, as said below
- keeper_position: int32 [256, 2048], P('axial', 'depth'), may hold values from 0 to 4095, as said below
Outputs:
- kelvin_after_step: float32 [256, 128, 2048], P('axial', 'depth')
- delivered_blowing: float32 [1048576], P(('axial', 'depth'))
The draws below stay inside these ranges and needn't reach their ends.
Inputs may be any that keep to these rules, and one draw needn't show every extreme that they name: `stream_keeper`: each flow owner takes the surface faces of one contiguous range of axial rows, the same at every azimuth; different owners take different ranges; every owner holds at least 8 rows and at most 32, and one owner holds exactly 32. `keeper_position`: within one azimuth slice of 128 columns, the faces of one owner hold the distinct slots 0 to their count - 1, in an order unrelated to position.
All inputs are finite; a program needn't handle non-finite values.
Results may differ from the reference program's by a relative error of at most 0.00014.
Values sent between devices are 32-bit elements; how exact they have to be, the bound alone decides.
No kernel may reach another device: no remote copies, remote signals or barrier semaphores. Data moves between devices by JAX's collectives and lax.ppermute only.
A program may use at most 128 MiB of HBM per device.

```python
import math
import jax
import jax.numpy as jnp

CA = 16
ROUND_SECTORS = 2048
NEWTON = 3
SWEEPS = 4
ZONES = 8
LENGTHWISE_ROWS = 256
THROUGH_LAYERS = 128
AZS = 128
OWN_CAP = 4096
SLOTS = 1048576
N_AXIAL = 16
N_DEPTH = 16


def owner_layout(key):
    base_key = jax.random.fold_in(key, 7)
    half_rows = CA // 2
    pair_count = (N_AXIAL - 3) // 2
    transfers = jax.random.randint(jax.random.fold_in(base_key, 2), (pair_count,), 0, half_rows + 1)
    lengths = jnp.full((N_AXIAL,), CA, jnp.int32)
    lengths = lengths.at[0].set(2 * CA).at[1].set(half_rows).at[2].set(half_rows)
    pair_first = 3 + 2 * jnp.arange(pair_count, dtype=jnp.int32)
    lengths = lengths.at[pair_first].add(-transfers).at[pair_first + 1].add(transfers)
    row_ends = jnp.cumsum(lengths)
    row_starts = row_ends - lengths
    row_count = CA * N_AXIAL
    row_ids = jnp.arange(row_count, dtype=jnp.int32)
    ranges = jnp.sum((row_ids[:, None] >= row_ends[None, :]).astype(jnp.int32), axis=1)
    face_count = row_count * AZS
    first_slot = row_starts[ranges] * AZS

    def one_slice(slice_number):
        shuffle_ids = jax.random.permutation(jax.random.fold_in(jax.random.fold_in(base_key, 3), slice_number), face_count)
        scores = ranges[:, None] * face_count + shuffle_ids.reshape(row_count, AZS)
        ranking = jnp.argsort(jnp.argsort(scores.reshape(-1), stable=True), stable=True).reshape(row_count, AZS)
        return ranking.astype(jnp.int32) - first_slot[:, None]
    slot_grid = jax.vmap(one_slice)(jnp.arange(N_DEPTH, dtype=jnp.int32))
    slot_grid = jnp.transpose(slot_grid, (1, 0, 2)).reshape(row_count, N_DEPTH * AZS)
    owner_order = jax.random.permutation(jax.random.fold_in(base_key, 4), N_AXIAL).astype(jnp.int32)
    owners = owner_order[ranges]
    owner_grid = jnp.broadcast_to(owners[:, None], (row_count, N_DEPTH * AZS))
    return (owner_grid.astype(jnp.int32), slot_grid.astype(jnp.int32))


def draw_stream_keeper(key, part):
    return owner_layout(key)[0]


def draw_keeper_position(key, part):
    return owner_layout(key)[1]


def plant(drawn, stream_key, smallest, largest):
    place = [jax.random.randint(jax.random.fold_in(stream_key, axis), (), 0, length) for axis, length in enumerate(drawn.shape)]
    widest = drawn.shape.index(max(drawn.shape))
    beside = place[:widest] + [(place[widest] + 1) % drawn.shape[widest]] + place[widest + 1:]
    return drawn.at[tuple(place)].set(smallest).at[tuple(beside)].set(largest)


def shard_levels(own_key, shape, split, low, top_value):
    gain, own = 1.0, jax.random.fold_in(own_key, 6)
    for axis_at, parts in split:
        steps = jnp.exp(jax.random.uniform(jax.random.fold_in(own, axis_at), (parts,), jnp.float32, low / len(split), top_value / len(split)))
        gain = gain * jnp.repeat(steps, shape[axis_at] // parts).reshape([-1 if axis == axis_at else 1 for axis in range(len(shape))])
    return gain


def gaussian(rng, shape, width, most, cuts=(), held_as=jnp.bfloat16):
    result = jax.random.normal(rng, shape, jnp.float32) * width
    if len(cuts) > 0:
        result = shard_levels(rng, shape, cuts, -0.22, 0.18) * result
    return jnp.clip(result, min=-most, max=most).astype(held_as)


def setup_inputs(seed: int = 0) -> dict:
    seeds = jax.random.split(jax.random.key(seed), 11)
    kelvin_before_step = gaussian(seeds[0], (LENGTHWISE_ROWS, THROUGH_LAYERS, ROUND_SECTORS), 0.5, 3.0, ((0, 16), (1, 16)), jnp.float32)
    unburnt_resin_share = jnp.clip(0.2 + 0.8 * jax.random.uniform(seeds[1], (LENGTHWISE_ROWS, THROUGH_LAYERS, ROUND_SECTORS), jnp.float32) ** shard_levels(seeds[1], (LENGTHWISE_ROWS, THROUGH_LAYERS, ROUND_SECTORS), ((0, 16), (1, 16)), -0.2, 0.2), 0.2, 1.0)
    deposited_energy_amount = gaussian(seeds[2], (LENGTHWISE_ROWS, THROUGH_LAYERS, ROUND_SECTORS), 1.0, 6.0, ((0, 16), (1, 16)), jnp.float32)
    material_label = plant(jax.random.randint(seeds[3], (LENGTHWISE_ROWS, THROUGH_LAYERS, ROUND_SECTORS), 0, ZONES), jax.random.fold_in(seeds[3], 1), 0, ZONES - 1).astype(jnp.int32)
    zonal_diffusivity = jnp.clip(jnp.exp(jax.random.uniform(seeds[4], (ZONES,), jnp.float32, math.log(0.5), math.log(2.0))), 0.5, 2.0)
    zonal_storage_coefficient = jnp.clip(jnp.exp(jax.random.uniform(seeds[5], (ZONES,), jnp.float32, math.log(0.05), math.log(0.5))), 0.05, 0.5)
    frequency_coefficient = jnp.clip(jnp.exp(jax.random.uniform(seeds[6], (ZONES,), jnp.float32, math.log(0.2), math.log(2.0))), 0.2, 2.0)
    arrhenius_barrier = jnp.clip(jax.random.uniform(seeds[7], (ZONES,), jnp.float32, 1.0, 4.0), 1.0, 4.0)
    stream_keeper = draw_stream_keeper(jax.random.fold_in(seeds[10], 71), 0)
    keeper_position = draw_keeper_position(jax.random.fold_in(seeds[10], 71), 0)
    return {"kelvin_before_step": kelvin_before_step, "unburnt_resin_share": unburnt_resin_share, "deposited_energy_amount": deposited_energy_amount, "material_label": material_label, "zonal_diffusivity": zonal_diffusivity, "zonal_storage_coefficient": zonal_storage_coefficient, "frequency_coefficient": frequency_coefficient, "arrhenius_barrier": arrhenius_barrier, "stream_keeper": stream_keeper, "keeper_position": keeper_position}


lengthwise_coupling_table = 1.0
circumferential_coupling_table = 1.0
layerwise_coupling_table = 2.0
charring_enthalpy = 0.5
outgassing_advection_enthalpy = 4.0


def nearby_volumes(spatial_array):
    bordered_kelvin_values = jnp.pad(spatial_array, ((1, 1), (1, 1), (0, 0)))
    lengthwise_couple = bordered_kelvin_values[2:, 1:-1] + bordered_kelvin_values[:-2, 1:-1]
    circumferential_couple = jnp.roll(spatial_array, 1, axis=2) + jnp.roll(spatial_array, -1, axis=2)
    return lengthwise_couple, circumferential_couple, bordered_kelvin_values[1:-1, 2:], bordered_kelvin_values[1:-1, :-2]


def charring_production(kelvin_after_step, frequency_coefficient_grid, arrhenius_barrier_grid, unburnt_resin_share):
    smoothed_kelvin_values = 1.0 + jnp.abs(kelvin_after_step)
    charring_speed = frequency_coefficient_grid * unburnt_resin_share * jnp.exp(arrhenius_barrier_grid * kelvin_after_step / smoothed_kelvin_values)
    speed_sensitivity = charring_speed * arrhenius_barrier_grid / (smoothed_kelvin_values * smoothed_kelvin_values)
    return charring_speed, speed_sensitivity


def reference(kelvin_before_step, unburnt_resin_share, deposited_energy_amount, material_label, zonal_diffusivity, zonal_storage_coefficient, frequency_coefficient, arrhenius_barrier, stream_keeper, keeper_position):
    transfer_coefficient = zonal_diffusivity[material_label]
    storage_coefficient = zonal_storage_coefficient[material_label]
    frequency_coefficient_grid = frequency_coefficient[material_label]
    arrhenius_barrier_grid = arrhenius_barrier[material_label]
    layer_spacing = 1.0 / THROUGH_LAYERS
    spokes = 2.0 * (lengthwise_coupling_table + circumferential_coupling_table + layerwise_coupling_table)
    kelvin_after_step = kelvin_before_step
    for iteration in range(NEWTON):
        charring_speed, speed_sensitivity = charring_production(kelvin_after_step, frequency_coefficient_grid, arrhenius_barrier_grid, unburnt_resin_share)
        outgassing_mass_stream = (jnp.sum(charring_speed, axis=1, keepdims=True) - jnp.cumsum(charring_speed, axis=1)) * layer_spacing
        lengthwise_couple, circumferential_couple, inward_layer_value, outward_layer_value = nearby_volumes(kelvin_after_step)
        iterative_mismatch = (storage_coefficient * (kelvin_after_step - kelvin_before_step)
                    - transfer_coefficient * (lengthwise_coupling_table * (lengthwise_couple - 2.0 * kelvin_after_step)
                                 + circumferential_coupling_table * (circumferential_couple - 2.0 * kelvin_after_step)
                                 + layerwise_coupling_table * (inward_layer_value + outward_layer_value - 2.0 * kelvin_after_step))
                    + charring_enthalpy * charring_speed + outgassing_advection_enthalpy * outgassing_mass_stream * (kelvin_after_step - inward_layer_value) - deposited_energy_amount)
        diagonal = storage_coefficient + transfer_coefficient * spokes + charring_enthalpy * speed_sensitivity + outgassing_advection_enthalpy * outgassing_mass_stream
        iterative_correction = jnp.zeros_like(kelvin_after_step)
        for sweep_index in range(SWEEPS):
            pair_a, pair_z, deeper_up, shallower_up = nearby_volumes(iterative_correction)
            iterative_correction = (-iterative_mismatch + transfer_coefficient * (lengthwise_coupling_table * pair_a + circumferential_coupling_table * pair_z
                                             + layerwise_coupling_table * (deeper_up + shallower_up))
                      + outgassing_advection_enthalpy * outgassing_mass_stream * deeper_up) / diagonal
        kelvin_after_step = kelvin_after_step + iterative_correction
    charring_speed, speed_sensitivity = charring_production(kelvin_after_step, frequency_coefficient_grid, arrhenius_barrier_grid, unburnt_resin_share)
    blowing = jnp.sum(charring_speed, axis=1) * layer_spacing
    column = jnp.arange(ROUND_SECTORS, dtype=jnp.int32) // AZS
    flat_index = (stream_keeper * N_DEPTH + column[None, :]) * OWN_CAP + keeper_position
    delivered_blowing = jnp.zeros((SLOTS,), jnp.float32).at[flat_index.reshape(-1)].set(blowing.reshape(-1))
    return kelvin_after_step, delivered_blowing
```

```python
import functools

import jax
import jax.numpy as jnp
from jax import lax
from jax.experimental import pallas as pl
from jax.experimental.pallas import tpu as pltpu
from jax.sharding import PartitionSpec as P

SWEEPS = 4
H = 4
W = 16
PAD = 8
LANES = 128
LO, HI = PAD, PAD + 2 * W + LANES
FULL = HI + PAD
CORE = slice(PAD + W, PAD + W + LANES)
VMEM_LIMIT = 56 * 1024 * 1024

VM = pl.BlockSpec(memory_space=pltpu.VMEM)
SM = pl.BlockSpec(memory_space=pltpu.SMEM)


def params():
    return pltpu.CompilerParams(vmem_limit_bytes=VMEM_LIMIT)


def f32(*shape):
    return jax.ShapeDtypeStruct(shape, jnp.float32)


def lane_iota(rows):
    return lax.broadcasted_iota(jnp.int32, (rows, LANES), 1)


def split3(x):
    a = x.astype(jnp.bfloat16)
    rest = x - a.astype(jnp.float32)
    b = rest.astype(jnp.bfloat16)
    c = (rest - b.astype(jnp.float32)).astype(jnp.bfloat16)
    return a, b, c


def edges_kernel(*refs):
    ins, out = refs[:-1], refs[-1]
    slices = out.shape[0]
    lane = lane_iota(8)

    def row(a, _):
        turned = [
            [
                pltpu.roll(
                    x[a, :, LANES * s : LANES * (s + 1)].astype(jnp.float32), (2 * W * i + W) % LANES, 1
                )
                for s in range(slices)
            ]
            for i, x in enumerate(ins)
        ]
        for s in range(slices):
            result = jnp.zeros((8, LANES), jnp.float32)
            for i in range(len(ins)):
                before, after = turned[i][s - 1], turned[i][(s + 1) % slices]
                result = jnp.where(lane >= 2 * W * i, before, result)
                result = jnp.where(lane >= 2 * W * i + W, after, result)
            out[s, a] = result
        return 0

    lax.fori_loop(0, out.shape[1], row, 0)


def suffix_matrix(m_ref):
    rows, cols = m_ref.shape
    source = lax.broadcasted_iota(jnp.int32, (rows, cols), 0) & (LANES - 1)
    target = lax.broadcasted_iota(jnp.int32, (rows, cols), 1)
    m_ref[...] = jnp.where(source > target, 4.0 / LANES, 0.0).astype(jnp.bfloat16)


def newton(first_row, total_rows, t, t0, conduct, capacity, act, pre, dep, m_ref, cs, cd, ua, ub, uc, finish):
    span = HI - LO
    lane = lane_iota(span)

    def setup(r, _):
        tc = t[r, LO:HI]
        a = act[r, LO:HI]
        q = 1.0 / (1.0 + jnp.abs(tc))
        aq = a * q
        p = pre[r, LO:HI] * jnp.exp(aq * tc)
        gas = jnp.dot(
            jnp.concatenate(split3(p), axis=1), m_ref[...], preferred_element_type=jnp.float32
        )
        c = conduct[r, LO:HI]
        cap = capacity[r, LO:HI]
        deeper = jnp.where(lane == LANES - 1, 0.0, pltpu.roll(tc, LANES - 1, 1))
        shallower = jnp.where(lane == 0, 0.0, pltpu.roll(tc, 1, 1))
        pairs = t[r - 1, LO:HI] + t[r + 1, LO:HI] + t[r, LO - 1 : HI - 1] + t[r, LO + 1 : HI + 1]
        spread = pairs + 2.0 * (deeper + shallower) - 8.0 * tc
        residual = (
            cap * (tc - t0[r, LO:HI])
            - c * spread
            + 0.5 * p
            + gas * (tc - deeper)
            - dep[r, LO:HI]
        )
        diagonal = cap + 8.0 * c + 0.5 * p * (aq * q) + gas
        row = first_row + r
        inside = jnp.where((row >= 0) & (row < total_rows), 1.0, 0.0)
        inverse = inside / diagonal
        ua[r, LO:HI] = -residual * inverse
        cs[r, LO:HI] = c * inverse
        cd[r, LO:HI] = jnp.where(lane == LANES - 1, 0.0, (2.0 * c + gas) * inverse)
        return 0

    rows = t.shape[0]
    lax.fori_loop(1, rows - 1, setup, 0)

    def swept(src, r):
        u = src[r, LO:HI]
        pairs = src[r - 1, LO:HI] + src[r + 1, LO:HI] + src[r, LO - 1 : HI - 1] + src[r, LO + 1 : HI + 1]
        shallower = jnp.where(lane == 0, 0.0, pltpu.roll(u, 1, 1))
        deeper = pltpu.roll(u, LANES - 1, 1)
        return ua[r, LO:HI] + cs[r, LO:HI] * (pairs + 2.0 * shallower) + cd[r, LO:HI] * deeper

    def to(dst, src):
        def one(r, _):
            dst[r, LO:HI] = swept(src, r)
            return 0

        return one

    lax.fori_loop(2, rows - 2, to(ub, ua), 0)
    lax.fori_loop(3, rows - 3, to(uc, ub), 0)

    def last(r, _):
        finish(r - H, t[r, LO:HI] + swept(uc, r))
        return 0

    lax.fori_loop(H, rows - H, last, 0)


def from_cells(ref, r):
    x = ref[:, r]
    return x.reshape(x.shape[0] * x.shape[1], LANES).T


def hand_on(out, up, down):
    own = out.shape[0]

    def finish(r, value):
        out[r] = value

        @pl.when(r >= own - H)
        def _():
            up[r - (own - H)] = value

        @pl.when(r < H)
        def _():
            down[r] = value

    return finish


def work_arrays(rows):
    return [pltpu.VMEM((rows, FULL, LANES), jnp.float32) for _ in range(5)] + [
        pltpu.VMEM((3 * LANES, LANES), jnp.bfloat16)
    ]


def first_kernel(total_rows, scalars, tables, *refs):
    inputs, refs = refs[:15], refs[15:]
    t0, conduct, capacity, act, pre, dep, out, up, down, cs, cd, ua, ub, uc, m_ref = refs
    suffix_matrix(m_ref)
    own = out.shape[0]
    span = HI - LO

    def unpack(which, offset):
        t_in, label_in, share_in, dep_in, edge_in = (inputs[3 * i + which] for i in range(5))

        def one(i, _):
            r = i + offset
            edges = from_cells(edge_in, i)

            def whole(ref, index):
                at = 2 * W * index
                return jnp.concatenate(
                    [edges[at : at + W], from_cells(ref, i), edges[at + W : at + 2 * W]], axis=0
                )

            t0[r, LO:HI] = whole(t_in, 0)
            dep[r, LO:HI] = whole(dep_in, 3)
            label = whole(label_in, 1)
            fields = [jnp.full((span, LANES), tables[f, 0], jnp.float32) for f in range(4)]
            for zone in range(1, tables.shape[1]):
                here = label == float(zone)
                fields = [jnp.where(here, tables[f, zone], x) for f, x in enumerate(fields)]
            conduct[r, LO:HI] = fields[0]
            capacity[r, LO:HI] = fields[1]
            pre[r, LO:HI] = fields[2] * whole(share_in, 2)
            act[r, LO:HI] = fields[3]
            return 0

        return one

    lax.fori_loop(0, own, unpack(0, H), 0)
    lax.fori_loop(0, H, unpack(1, 0), 0)
    lax.fori_loop(0, H, unpack(2, own + H), 0)
    newton(
        scalars[0] * own - H, total_rows, t0, t0, conduct, capacity, act, pre, dep, m_ref,
        cs, cd, ua, ub, uc, hand_on(out, up, down),
    )


def spread_rows(t, own_t, above, below):
    own = own_t.shape[0]
    t[0:H, LO:HI] = above[...]
    t[H : H + own, LO:HI] = own_t[...]
    t[H + own :, LO:HI] = below[...]


def second_kernel(total_rows, scalars, own_t, above, below, t0, conduct, capacity, act, pre, dep, *refs):
    out, up, down, cs, cd, ua, ub, uc, m_ref, t = refs
    suffix_matrix(m_ref)
    spread_rows(t, own_t, above, below)
    newton(
        scalars[0] * out.shape[0] - H, total_rows, t, t0, conduct, capacity, act, pre, dep, m_ref,
        cs, cd, ua, ub, uc, hand_on(out, up, down),
    )


def third_kernel(total_rows, scalars, own_t, above, below, t0, conduct, capacity, act, pre, dep, *refs):
    out, blowing, cs, cd, ua, ub, uc, m_ref, t = refs
    suffix_matrix(m_ref)
    spread_rows(t, own_t, above, below)

    def finish(r, value):
        value = value[W : W + LANES]
        out[:, r] = value.T.reshape(out.shape[0], 8, LANES)
        p = pre[r + H, CORE] * jnp.exp(act[r + H, CORE] * value / (1.0 + jnp.abs(value)))
        blowing[pl.ds(r, 1), :] = jnp.sum(p.T, axis=0, keepdims=True) * (1.0 / LANES)

    newton(
        scalars[0] * out.shape[1] - H, total_rows, t, t0, conduct, capacity, act, pre, dep, m_ref,
        cs, cd, ua, ub, uc, finish,
    )


def deliver_kernel(scalars, gathered, out, left, right):
    groups, rows3, _ = gathered.shape
    rows = rows3 // 3
    me = scalars[0]
    owners = gathered[:, 2 * rows :, :].astype(jnp.int32)
    shape = owners.shape
    number = lax.broadcasted_iota(jnp.int32, shape, 0) * rows + lax.broadcasted_iota(jnp.int32, shape, 1)
    first = jnp.min(jnp.where(owners == me, number, groups * rows))
    most = out.shape[0]
    first = jnp.minimum(first, groups * rows - most)
    high_of = lax.broadcasted_iota(jnp.int32, (most, LANES), 0)
    low_of = lax.broadcasted_iota(jnp.int32, (LANES, LANES), 0)
    for i in range(most):
        at = first + i
        group, r = at // rows, at % rows
        value = gathered[group, pl.ds(r, 1), :]
        slot = gathered[group, pl.ds(rows + r, 1), :].astype(jnp.int32)
        owner = gathered[group, pl.ds(2 * rows + r, 1), :].astype(jnp.int32)
        high = jnp.where(owner == me, slot >> 7, -1)
        low = slot & (LANES - 1)
        here = slice(LANES * i, LANES * (i + 1))
        hit = high_of == high
        for k, part in enumerate(split3(value)):
            left[most * k : most * (k + 1), here] = jnp.where(hit, part.astype(jnp.float32), 0.0).astype(
                jnp.bfloat16
            )
        right[:, here] = jnp.where(low_of == low, 1.0, 0.0).astype(jnp.bfloat16)
    parts = lax.dot_general(
        left[...], right[...], (((1,), (1,)), ((), ())), preferred_element_type=jnp.float32
    )
    out[...] = parts[:most] + parts[most : 2 * most] + parts[2 * most :]


def shards(
    kelvin_before_step,
    unburnt_resin_share,
    deposited_energy_amount,
    material_label,
    zonal_diffusivity,
    zonal_storage_coefficient,
    frequency_coefficient,
    arrhenius_barrier,
    stream_keeper,
    keeper_position,
):
    own, layers, columns = kelvin_before_step.shape
    n_axial, n_depth = lax.axis_size("axial"), lax.axis_size("depth")
    place = lax.axis_index("axial").astype(jnp.int32).reshape(1)
    total_rows = own * n_axial
    label = material_label.astype(jnp.float32)
    tables = jnp.stack(
        [zonal_diffusivity, zonal_storage_coefficient, frequency_coefficient, arrhenius_barrier]
    )

    edges = pl.pallas_call(
        edges_kernel,
        out_shape=f32(n_depth, own, layers, LANES),
        in_specs=[VM] * 4,
        out_specs=VM,
        compiler_params=params(),
        name="edges",
    )(kelvin_before_step, material_label, unburnt_resin_share, deposited_energy_amount)

    def packed(x):
        return jnp.transpose(x.reshape(own, layers, n_depth, LANES), (2, 0, 1, 3))

    def up(x):
        return lax.ppermute(x, "axial", [(i, i + 1) for i in range(n_axial - 1)])

    def down(x):
        return lax.ppermute(x, "axial", [(i + 1, i) for i in range(n_axial - 1)])

    operands = []
    for x in (packed(kelvin_before_step), packed(label), packed(unburnt_resin_share),
              packed(deposited_energy_amount), edges):
        y = lax.all_to_all(x, "depth", 0, 0)
        operands += [y, up(y[:, own - H :]), down(y[:, :H])]

    extended = f32(own + 2 * H, FULL, LANES)
    block = f32(own, HI - LO, LANES)
    rim = f32(H, HI - LO, LANES)
    *state, t, above, below = pl.pallas_call(
        functools.partial(first_kernel, total_rows),
        out_shape=[extended] * 6 + [block, rim, rim],
        in_specs=[SM, SM] + [VM] * 15,
        out_specs=[VM] * 9,
        scratch_shapes=work_arrays(own + 2 * H),
        compiler_params=params(),
        name="newton1",
    )(place, tables, *operands)
    t, above, below = pl.pallas_call(
        functools.partial(second_kernel, total_rows),
        out_shape=[block, rim, rim],
        in_specs=[SM] + [VM] * 9,
        out_specs=[VM] * 3,
        scratch_shapes=work_arrays(own + 2 * H) + [pltpu.VMEM((own + 2 * H, FULL, LANES), jnp.float32)],
        compiler_params=params(),
        name="newton2",
    )(place, t, up(above), down(below), *state)
    kelvin, blowing = pl.pallas_call(
        functools.partial(third_kernel, total_rows),
        out_shape=[f32(n_depth, own, layers, LANES), f32(own, LANES)],
        in_specs=[SM] + [VM] * 9,
        out_specs=[VM] * 2,
        scratch_shapes=work_arrays(own + 2 * H) + [pltpu.VMEM((own + 2 * H, FULL, LANES), jnp.float32)],
        compiler_params=params(),
        name="newton3",
    )(place, t, up(above), down(below), *state)

    kelvin = lax.all_to_all(kelvin, "depth", 0, 0)
    kelvin = jnp.transpose(kelvin, (1, 2, 0, 3)).reshape(own, layers, columns)

    faces = jnp.concatenate(
        [blowing, keeper_position.astype(jnp.float32), stream_keeper.astype(jnp.float32)], axis=0
    )
    gathered = lax.all_gather(faces, "axial")
    slots = 2 * own * LANES
    delivered = pl.pallas_call(
        deliver_kernel,
        out_shape=f32(slots // LANES, LANES),
        in_specs=[SM, VM],
        out_specs=VM,
        scratch_shapes=[
            pltpu.VMEM((3 * slots // LANES, slots), jnp.bfloat16),
            pltpu.VMEM((LANES, slots), jnp.bfloat16),
        ],
        compiler_params=params(),
        name="deliver",
    )(place, gathered)
    return (kelvin, delivered.reshape(slots))


def solution(mesh):
    cells = P("axial", "depth", None)
    faces = P("axial", "depth")
    return jax.shard_map(
        shards,
        mesh=mesh,
        in_specs=(cells, cells, cells, cells, P(), P(), P(), P(), faces, faces),
        out_specs=(cells, P(("axial", "depth"))),
        check_vma=False,
    )
```

```python
import functools

import jax
import jax.numpy as jnp
from jax import lax
from jax.experimental import pallas as pl
from jax.experimental.pallas import tpu as pltpu
from jax.sharding import PartitionSpec as P

SWEEPS = 4
H = 4
W = 16
PAD = 8
LANES = 128
WIDE = (PAD, PAD + 2 * W + LANES)
NEAR = (PAD + W // 2, PAD + W + LANES + W // 2)
CORE = (PAD + W, PAD + W + LANES)
FULL = WIDE[1] + PAD
VMEM_LIMIT = 12 * 1024 * 1024

VM = pl.BlockSpec(memory_space=pltpu.VMEM)
SM = pl.BlockSpec(memory_space=pltpu.SMEM)


def f32(*shape):
    return jax.ShapeDtypeStruct(shape, jnp.float32)


def call(kernel, name, scalars, reads, updates, makes, scratch=(), kept=True, space=pltpu.VMEM):
    counts = [len(scalars), len(reads), len(updates), len(updates), len(makes), len(scratch)]

    def body(*refs):
        groups, at = [], 0
        for count in counts:
            groups.append(refs[at : at + count])
            at += count
        kernel(groups[0], groups[1], groups[3], groups[4], groups[5])

    first = len(scalars) + len(reads)
    results = pl.pallas_call(
        body,
        out_shape=[pltpu.VMEM(u.shape, jnp.float32) for u in updates]
        + [pltpu.VMEM(s, jnp.float32) if kept else f32(*s) for s in makes],
        in_specs=[SM] * len(scalars)
        + [pl.BlockSpec(memory_space=space)] * len(reads)
        + [VM] * len(updates),
        out_specs=[VM] * (len(updates) + len(makes)),
        input_output_aliases={first + i: i for i in range(len(updates))},
        scratch_shapes=list(scratch),
        compiler_params=pltpu.CompilerParams(vmem_limit_bytes=VMEM_LIMIT),
        name=name,
    )(*scalars, *reads, *updates)
    return list(results)


def lane_iota(rows):
    return lax.broadcasted_iota(jnp.int32, (rows, LANES), 1)


def split3(x):
    a = x.astype(jnp.bfloat16)
    rest = x - a.astype(jnp.float32)
    b = rest.astype(jnp.bfloat16)
    c = (rest - b.astype(jnp.float32)).astype(jnp.bfloat16)
    return a, b, c


def over(ranges, body):
    for low, high in ranges:
        for r in range(low, high):
            body(r)


def pack_kernel(scalars, ins, updates, makes, scratch):
    (out,), held, sems = makes, scratch[:-1], scratch[-1]
    slices = out.shape[0]
    own = ins[0].shape[0]
    lane = lane_iota(8)
    copies = [pltpu.make_async_copy(x, y, sems.at[i]) for i, (x, y) in enumerate(zip(ins, held))]
    for copy in copies:
        copy.start()

    def spread(i):
        def row(a, _):
            for s in range(slices):
                out[s, i * own + a] = held[i][a, :, LANES * s : LANES * (s + 1)].astype(jnp.float32)
            return 0

        return row

    for i, copy in enumerate(copies):
        copy.wait()
        lax.fori_loop(0, own, spread(i), 0, unroll=4)

    def rims(a, _):
        turned = [
            [
                pltpu.roll(
                    x[a, :, LANES * s : LANES * (s + 1)].astype(jnp.float32), (2 * W * i + W) % LANES, 1
                )
                for s in range(slices)
            ]
            for i, x in enumerate(held)
        ]
        for s in range(slices):
            result = turned[0][s - 1]
            for i in range(len(ins)):
                if i:
                    result = jnp.where(lane >= 2 * W * i, turned[i][s - 1], result)
                result = jnp.where(lane >= 2 * W * i + W, turned[i][(s + 1) % slices], result)
            out[s, len(ins) * own + a] = result
        return 0

    lax.fori_loop(0, own, rims, 0)


def rim_rows(kind):
    return H if kind in (0, 4) else H - 1


def rim_start(kind):
    return sum(rim_rows(k) for k in range(kind))


def rims_kernel(scalars, reads, updates, makes, scratch):
    (arrived,), (top, bottom) = reads, makes
    own = arrived.shape[1] // 5
    for kind in range(5):
        count, at = rim_rows(kind), rim_start(kind)
        bottom[:, at : at + count] = arrived[:, kind * own : kind * own + count]
        top[:, at : at + count] = arrived[:, (kind + 1) * own - count : (kind + 1) * own]


def suffix_matrix(m_ref):
    rows, cols = m_ref.shape
    source = lax.broadcasted_iota(jnp.int32, (rows, cols), 0) & (LANES - 1)
    target = lax.broadcasted_iota(jnp.int32, (rows, cols), 1)
    m_ref[...] = jnp.where(source > target, 4.0 / LANES, 0.0).astype(jnp.bfloat16)


def linearise(r, row, total_rows, span, t, t0, fields, m_ref):
    lo, hi = span
    conduct, capacity, act, pre = fields
    lane = lane_iota(hi - lo)
    tc = t[r, lo:hi]
    a = act[r, lo:hi]
    q = 1.0 / (1.0 + jnp.abs(tc))
    aq = a * q
    p = pre[r, lo:hi] * jnp.exp(aq * tc)
    gas = jnp.dot(jnp.concatenate(split3(p), axis=1), m_ref[...], preferred_element_type=jnp.float32)
    c = conduct[r, lo:hi]
    cap = capacity[r, lo:hi]
    deeper = jnp.where(lane == LANES - 1, 0.0, pltpu.roll(tc, LANES - 1, 1))
    shallower = jnp.where(lane == 0, 0.0, pltpu.roll(tc, 1, 1))
    pairs = t[r - 1, lo:hi] + t[r + 1, lo:hi] + t[r, lo - 1 : hi - 1] + t[r, lo + 1 : hi + 1]
    spread = pairs + 2.0 * (deeper + shallower) - 8.0 * tc
    source = c * spread - 0.5 * p - gas * (tc - deeper)
    if t0 is not None:
        source = source - cap * (tc - t0[r, lo:hi])
    diagonal = cap + 8.0 * c + 0.5 * p * (aq * q) + gas
    inside = jnp.where((row >= 0) & (row < total_rows), 1.0, 0.0)
    inverse = inside / diagonal
    return source, inverse, c * inverse, jnp.where(lane == LANES - 1, 0.0, (2.0 * c + gas) * inverse)


def sweeps(span, work, ranges, finish):
    lo, hi = span
    first, side, down, b, c = work
    lane = lane_iota(hi - lo)

    def swept(src, r):
        u = src[r, lo:hi]
        pairs = src[r - 1, lo:hi] + src[r + 1, lo:hi] + src[r, lo - 1 : hi - 1] + src[r, lo + 1 : hi + 1]
        shallower = jnp.where(lane == 0, 0.0, pltpu.roll(u, 1, 1))
        deeper = pltpu.roll(u, LANES - 1, 1)
        return first[r, lo:hi] + side[r, lo:hi] * (pairs + 2.0 * shallower) + down[r, lo:hi] * deeper

    def second(r):
        b[r, lo:hi] = swept(first, r)

    def third(r):
        c[r, lo:hi] = swept(b, r)

    over(ranges[0], second)
    over(ranges[1], third)
    over(ranges[2], lambda r: finish(r, swept(c, r)))


def inner_rows(rows, k):
    return [(H + k, rows - H - k)]


def outer_rows(rows, k):
    return [(k, H + k), (rows - H - k, rows - k)]


def from_cells(ref, r):
    x = ref[:, r]
    return x.reshape(x.shape[0] * x.shape[1], LANES).T


def unpack_row(tables, arrived, at, r, state):
    t0, conduct, capacity, act, pre, dep = state
    lo, hi = WIDE
    edges = from_cells(arrived, at[4])

    def whole(kind):
        e = 2 * W * kind
        return jnp.concatenate(
            [edges[e : e + W], from_cells(arrived, at[kind]), edges[e + W : e + 2 * W]], axis=0
        )

    t0[r, lo:hi] = whole(0)
    if at[1] is None:
        return
    label = whole(1)
    fields = [jnp.full(label.shape, tables[f, 0], jnp.float32) for f in range(4)]
    for zone in range(1, tables.shape[1]):
        here = label == float(zone)
        fields = [jnp.where(here, tables[f, zone], x) for f, x in enumerate(fields)]
    conduct[r, lo:hi] = fields[0]
    capacity[r, lo:hi] = fields[1]
    pre[r, lo:hi] = fields[2] * whole(2)
    act[r, lo:hi] = fields[3]
    dep[r, lo:hi] = whole(3)


def keeper(span, t, t_new, rims):
    lo, hi = span
    own = t.shape[0] - 2 * H

    def finish(r, update):
        value = (t[r, lo:hi] + update)[NEAR[0] - lo : NEAR[1] - lo]
        t_new[r, slice(*NEAR)] = value
        if rims is not None and r >= own:
            rims[0][r - own] = value
        if rims is not None and r < 2 * H:
            rims[1][r - H] = value

    return finish


def first_kernel(outer, total_rows, scalars, reads, updates, makes, scratch):
    place, tables = scalars
    arrays, rims = (updates, makes) if outer else (makes, None)
    state, (ua, cs, cd, ub, uc, t_new) = arrays[:6], arrays[6:]
    t0, conduct, capacity, act, pre, dep = state
    rows = t0.shape[0]
    own = rows - 2 * H
    suffix_matrix(scratch[0])
    if outer:
        for i in range(H):
            for ref, r, missing in ((reads[0], i, i == 0), (reads[1], i + H + own, i == H - 1)):
                skip = H if ref is reads[0] else 0
                at = [rim_start(k) + (i - (H - rim_rows(k)) if skip else i) for k in range(5)]
                if missing:
                    at[1:4] = [None] * 3
                unpack_row(tables, ref, at, r, state)
    else:
        for i in range(own):
            unpack_row(tables, reads[0], [k * own + i for k in range(5)], i + H, state)
    lo, hi = WIDE

    def one(r):
        source, inverse, side, down = linearise(
            r, place[0] * own + r - H, total_rows, WIDE, t0, None, (conduct, capacity, act, pre), scratch[0]
        )
        ua[r, lo:hi] = (source + dep[r, lo:hi]) * inverse
        cs[r, lo:hi] = side
        cd[r, lo:hi] = down

    ranges = outer_rows if outer else inner_rows
    over(ranges(rows, 1), one)
    sweeps(WIDE, (ua, cs, cd, ub, uc), [ranges(rows, k) for k in (2, 3, 4)], keeper(WIDE, t0, t_new, rims))


def later_kernel(outer, last, total_rows, scalars, reads, updates, makes, scratch):
    (place,) = scalars
    lo, hi = NEAR
    if outer:
        above, below, t0, conduct, capacity, act, pre, dep = reads[:8]
        t, ua, cs, cd, ub, uc = updates[:6]
        results, rims = (makes, None) if last else (updates[6:], makes)
    else:
        t, t0, conduct, capacity, act, pre, dep = reads
        ua, cs, cd, ub, uc = makes[:5]
        results, rims = makes[5:], None
    rows = t0.shape[0]
    own = rows - 2 * H
    suffix_matrix(scratch[0])
    if outer:
        t[0:H, lo:hi] = above[...]
        t[H + own :, lo:hi] = below[...]

    def one(r):
        source, inverse, side, down = linearise(
            r, place[0] * own + r - H, total_rows, NEAR, t, t0, (conduct, capacity, act, pre), scratch[0]
        )
        ua[r, lo:hi] = (source + dep[r, lo:hi]) * inverse
        cs[r, lo:hi] = side
        cd[r, lo:hi] = down

    if last:
        out, blowing = results
        if outer:
            out[...], blowing[...] = reads[8][...], reads[9][...]
        core = slice(*CORE)
        mid = slice(CORE[0] - lo, CORE[1] - lo)

        def finish(r, update):
            value = t[r, core] + update[mid]
            out[:, r - H] = value.T.reshape(out.shape[0], 8, LANES)
            p = pre[r, core] * jnp.exp(act[r, core] * value / (1.0 + jnp.abs(value)))
            blowing[r - H : r - H + 1, :] = jnp.sum(p.T, axis=0, keepdims=True) * (1.0 / LANES)

    else:
        finish = keeper(NEAR, t, results[0], rims)
    ranges = outer_rows if outer else inner_rows
    over(ranges(rows, 1), one)
    sweeps(NEAR, (ua, cs, cd, ub, uc), [ranges(rows, k) for k in (2, 3, 4)], finish)


def deliver_kernel(scalars, reads, updates, makes, scratch):
    (gathered,), (out,), (left, right) = reads, makes, scratch
    groups, rows3, _ = gathered.shape
    rows = rows3 // 3
    me = scalars[0][0]
    owners = gathered[:, 2 * rows :, :].astype(jnp.int32)
    shape = owners.shape
    number = lax.broadcasted_iota(jnp.int32, shape, 0) * rows + lax.broadcasted_iota(jnp.int32, shape, 1)
    first = jnp.min(jnp.where(owners == me, number, groups * rows))
    most = out.shape[0]
    first = jnp.minimum(first, groups * rows - most)
    high_of = lax.broadcasted_iota(jnp.int32, (most, LANES), 0)
    low_of = lax.broadcasted_iota(jnp.int32, (LANES, LANES), 0)
    for i in range(most):
        at = first + i
        group, r = at // rows, at % rows
        value = gathered[group, pl.ds(r, 1), :]
        slot = gathered[group, pl.ds(rows + r, 1), :].astype(jnp.int32)
        owner = gathered[group, pl.ds(2 * rows + r, 1), :].astype(jnp.int32)
        high = jnp.where(owner == me, slot >> 7, -1)
        low = slot & (LANES - 1)
        here = slice(LANES * i, LANES * (i + 1))
        hit = high_of == high
        for k, part in enumerate(split3(value)):
            left[most * k : most * (k + 1), here] = jnp.where(hit, part.astype(jnp.float32), 0.0).astype(
                jnp.bfloat16
            )
        right[:, here] = jnp.where(low_of == low, 1.0, 0.0).astype(jnp.bfloat16)
    parts = lax.dot_general(
        left[...], right[...], (((1,), (1,)), ((), ())), preferred_element_type=jnp.float32
    )
    out[...] = parts[:most] + parts[most : 2 * most] + parts[2 * most :]


def shards(
    kelvin_before_step,
    unburnt_resin_share,
    deposited_energy_amount,
    material_label,
    zonal_diffusivity,
    zonal_storage_coefficient,
    frequency_coefficient,
    arrhenius_barrier,
    stream_keeper,
    keeper_position,
):
    own, layers, columns = kelvin_before_step.shape
    n_axial, n_depth = lax.axis_size("axial"), lax.axis_size("depth")
    place = lax.axis_index("axial").astype(jnp.int32).reshape(1)
    total_rows = own * n_axial
    tables = jnp.stack(
        [zonal_diffusivity, zonal_storage_coefficient, frequency_coefficient, arrhenius_barrier]
    )
    rows = own + 2 * H
    extended = (rows, FULL, LANES)
    rim = (H, NEAR[1] - NEAR[0], LANES)
    matrix = [pltpu.VMEM((3 * LANES, LANES), jnp.bfloat16)]

    def up(x):
        return lax.ppermute(x, "axial", [(i, i + 1) for i in range(n_axial - 1)])

    def down(x):
        return lax.ppermute(x, "axial", [(i + 1, i) for i in range(n_axial - 1)])

    cells = [kelvin_before_step, material_label, unburnt_resin_share, deposited_energy_amount]
    (sent,) = call(
        pack_kernel, "pack", [], cells, [], [(n_depth, 5 * own, layers, LANES)],
        [pltpu.VMEM(x.shape, x.dtype) for x in cells] + [pltpu.SemaphoreType.DMA((4,))],
        kept=False, space=pltpu.HBM,
    )
    arrived = lax.all_to_all(sent, "depth", 0, 0)
    top, bottom = call(
        rims_kernel, "rims", [], [arrived], [], [(n_depth, rim_start(5), layers, LANES)] * 2
    )
    above, below = up(top), down(bottom)
    arrays = call(
        functools.partial(first_kernel, False, total_rows), "newton1_inner",
        [place, tables], [arrived], [], [extended] * 12, matrix,
    )
    *arrays, top, bottom = call(
        functools.partial(first_kernel, True, total_rows), "newton1_outer",
        [place, tables], [above, below], arrays, [rim] * 2, matrix,
    )
    t0, conduct, capacity, act, pre, dep = arrays[:6]
    t = arrays[-1]
    for last in (False, True):
        above, below = up(top), down(bottom)
        fixed = [t0, conduct, capacity, act, pre, dep]
        results = [(n_depth, own, layers, LANES), (own, LANES)] if last else [extended]
        work = call(
            functools.partial(later_kernel, False, last, total_rows), "newton3_inner" if last else "newton2_inner",
            [place], [t] + fixed, [], [extended] * 5 + results, matrix,
        )
        work, results = work[:5], work[5:]
        work = call(
            functools.partial(later_kernel, True, last, total_rows), "newton3_outer" if last else "newton2_outer",
            [place], [above, below] + fixed + (results if last else []), [t] + work + ([] if last else results),
            [(n_depth, own, layers, LANES), (own, LANES)] if last else [rim] * 2, matrix, kept=not last,
        )
        if not last:
            t, top, bottom = work[6:]
    kelvin, blowing = work[6:]

    kelvin = lax.all_to_all(kelvin, "depth", 0, 0)
    kelvin = jnp.transpose(kelvin, (1, 2, 0, 3)).reshape(own, layers, columns)

    faces = jnp.concatenate(
        [blowing, keeper_position.astype(jnp.float32), stream_keeper.astype(jnp.float32)], axis=0
    )
    gathered = lax.all_gather(faces, "axial")
    slots = 2 * own * LANES
    (delivered,) = call(
        deliver_kernel, "deliver", [place], [gathered], [], [(slots // LANES, LANES)],
        [
            pltpu.VMEM((3 * slots // LANES, slots), jnp.bfloat16),
            pltpu.VMEM((LANES, slots), jnp.bfloat16),
        ],
        kept=False,
    )
    return (kelvin, delivered.reshape(slots))


def solution(mesh):
    cells = P("axial", "depth", None)
    faces = P("axial", "depth")
    return jax.shard_map(
        shards,
        mesh=mesh,
        in_specs=(cells, cells, cells, cells, P(), P(), P(), P(), faces, faces),
        out_specs=(cells, P(("axial", "depth"))),
        check_vma=False,
    )
```

```python
import functools

import jax
import jax.numpy as jnp
from jax import lax
from jax.experimental import pallas as pl
from jax.experimental.pallas import tpu as pltpu
from jax.sharding import PartitionSpec as P

SWEEPS = 4
H = 4
W = 16
LANES = 128
FULL = 2 * W + LANES
WIDE = (0, FULL)
NEAR = (W // 2, FULL - W // 2)
CORE = (W, W + LANES)

VM = pl.BlockSpec(memory_space=pltpu.VMEM)
SM = pl.BlockSpec(memory_space=pltpu.SMEM)


def f32(*shape):
    return jax.ShapeDtypeStruct(shape, jnp.float32)


def call(kernel, name, scalars, reads, updates, makes, scratch=(), kept=True, space=pltpu.VMEM, out_space=pltpu.VMEM, limit=8):
    counts = [len(scalars), len(reads), len(updates), len(updates), len(makes), len(scratch)]

    def body(*refs):
        groups, at = [], 0
        for count in counts:
            groups.append(refs[at : at + count])
            at += count
        kernel(groups[0], groups[1], groups[3], groups[4], groups[5])

    first = len(scalars) + len(reads)
    results = pl.pallas_call(
        body,
        out_shape=[pltpu.VMEM(u.shape, jnp.float32) for u in updates]
        + [out_space(s, jnp.float32) if kept else f32(*s) for s in makes],
        in_specs=[SM] * len(scalars)
        + [pl.BlockSpec(memory_space=space)] * len(reads)
        + [VM] * len(updates),
        out_specs=[VM] * len(updates) + [pl.BlockSpec(memory_space=out_space)] * len(makes),
        input_output_aliases={first + i: i for i in range(len(updates))},
        scratch_shapes=list(scratch),
        compiler_params=pltpu.CompilerParams(vmem_limit_bytes=limit * 1024 * 1024),
        name=name,
    )(*scalars, *reads, *updates)
    return list(results)


def lane_iota(rows):
    return lax.broadcasted_iota(jnp.int32, (rows, LANES), 1)


def split3(x):
    a = x.astype(jnp.bfloat16)
    rest = x - a.astype(jnp.float32)
    b = rest.astype(jnp.bfloat16)
    c = (rest - b.astype(jnp.float32)).astype(jnp.bfloat16)
    return a, b, c


def over(ranges, body):
    for low, high in ranges:
        for r in range(low, high):
            body(r)


def rim_rows(kind):
    return H if kind in (0, 4) else H - 1


def planes(first, own):
    if first:
        low = [(k, r) for k in range(5) for r in range(rim_rows(k))]
        high = [(k, r) for k in range(5) for r in range(own - rim_rows(k), own)]
        return low + high
    return [(k, r) for k in range(5) for r in range(rim_rows(k), own - rim_rows(k))]


def pack_kernel(first, scalars, ins, updates, makes, scratch):
    (result,), held, out, sems, out_sems = makes, scratch[:4], scratch[4], scratch[5], scratch[6]
    slices = out.shape[0]
    own = ins[0].shape[0]
    lane = lane_iota(8)
    bands = [slice(0, H), slice(own - H, own)] if first else [slice(H - 1, own - H + 1)]
    copies = [
        pltpu.make_async_copy(x.at[band], y.at[band], sems.at[i, j])
        for i, (x, y) in enumerate(zip(ins, held))
        for j, band in enumerate(bands)
    ]
    for copy in copies:
        copy.start()
    for copy in copies:
        copy.wait()

    def tile(k, a, s):
        return held[k][a, :, LANES * s : LANES * (s + 1)].astype(jnp.float32)

    order = planes(first, own)
    sent = []
    for p, (kind, a) in enumerate(order):
        if kind < 4:
            for s in range(slices):
                out[s, p] = tile(kind, a, s)
        else:
            turned = [
                [pltpu.roll(tile(k, a, s), (2 * W * k + W) % LANES, 1) for s in range(slices)] for k in range(4)
            ]
            for s in range(slices):
                value = turned[0][s - 1]
                for k in range(4):
                    if k:
                        value = jnp.where(lane >= 2 * W * k, turned[k][s - 1], value)
                    value = jnp.where(lane >= 2 * W * k + W, turned[k][(s + 1) % slices], value)
                out[s, p] = value
        if p + 1 == len(order) or order[p + 1][0] != kind:
            begin = sent[-1][1] if sent else 0
            band = slice(begin, p + 1)
            sent.append((pltpu.make_async_copy(out.at[:, band], result.at[:, band], out_sems.at[len(sent)]), p + 1))
            sent[-1][0].start()
    for copy, _ in sent:
        copy.wait()


def rims_kernel(scalars, reads, updates, makes, scratch):
    (arrived,), (top, bottom) = reads, makes
    count = top.shape[1]
    bottom[...] = arrived[:, :count]
    top[...] = arrived[:, count:]


def suffix_matrix(m_ref):
    rows, cols = m_ref.shape
    source = lax.broadcasted_iota(jnp.int32, (rows, cols), 0) & (LANES - 1)
    target = lax.broadcasted_iota(jnp.int32, (rows, cols), 1)
    m_ref[...] = jnp.where(source > target, 4.0 / LANES, 0.0).astype(jnp.bfloat16)


def azimuth_pair(ref, r, span):
    lo, hi = span
    if span == WIDE:
        x = ref[r]
        return pltpu.roll(x, 1, 0) + pltpu.roll(x, FULL - 1, 0)
    return ref[r, lo - 1 : hi - 1] + ref[r, lo + 1 : hi + 1]


def linearise(r, row, total_rows, span, t, t0, fields, m_ref):
    lo, hi = span
    conduct, capacity, act, pre = fields
    lane = lane_iota(hi - lo)
    tc = t[r, lo:hi]
    a = act[r, lo:hi]
    q = 1.0 / (1.0 + jnp.abs(tc))
    aq = a * q
    p = pre[r, lo:hi] * jnp.exp(aq * tc)
    gas = jnp.dot(jnp.concatenate(split3(p), axis=1), m_ref[...], preferred_element_type=jnp.float32)
    c = conduct[r, lo:hi]
    cap = capacity[r, lo:hi]
    deeper = jnp.where(lane == LANES - 1, 0.0, pltpu.roll(tc, LANES - 1, 1))
    shallower = jnp.where(lane == 0, 0.0, pltpu.roll(tc, 1, 1))
    pairs = t[r - 1, lo:hi] + t[r + 1, lo:hi] + azimuth_pair(t, r, span)
    spread = pairs + 2.0 * (deeper + shallower) - 8.0 * tc
    source = c * spread - 0.5 * p - gas * (tc - deeper)
    if t0 is not None:
        source = source - cap * (tc - t0[r, lo:hi])
    diagonal = cap + 8.0 * c + 0.5 * p * (aq * q) + gas
    inside = jnp.where((row >= 0) & (row < total_rows), 1.0, 0.0)
    inverse = inside / diagonal
    return source, inverse, c * inverse, jnp.where(lane == LANES - 1, 0.0, (2.0 * c + gas) * inverse)


def sweeps(span, work, ranges, finish):
    lo, hi = span
    first, side, down, b, c = work
    lane = lane_iota(hi - lo)

    def swept(src, r):
        u = src[r, lo:hi]
        pairs = src[r - 1, lo:hi] + src[r + 1, lo:hi] + azimuth_pair(src, r, span)
        shallower = jnp.where(lane == 0, 0.0, pltpu.roll(u, 1, 1))
        deeper = pltpu.roll(u, LANES - 1, 1)
        return first[r, lo:hi] + side[r, lo:hi] * (pairs + 2.0 * shallower) + down[r, lo:hi] * deeper

    def second(r):
        b[r, lo:hi] = swept(first, r)

    def third(r):
        c[r, lo:hi] = swept(b, r)

    over(ranges[0], second)
    over(ranges[1], third)
    over(ranges[2], lambda r: finish(r, swept(c, r)))


def inner_rows(rows, k):
    return [(H + k, rows - H - k)]


def outer_rows(rows, k):
    return [(k, H + k), (rows - H - k, rows - k)]


def from_cells(ref, r):
    x = ref[:, r]
    return x.reshape(x.shape[0] * x.shape[1], LANES).T


def unpack_row(tables, source, r, state):
    t0, conduct, capacity, act, pre, dep = state
    lo, hi = WIDE
    edges = from_cells(*source(4))

    def whole(kind):
        e = 2 * W * kind
        return jnp.concatenate(
            [edges[e : e + W], from_cells(*source(kind)), edges[e + W : e + 2 * W]], axis=0
        )

    t0[r, lo:hi] = whole(0)
    if source(1) is None:
        return
    label = whole(1)
    fields = [jnp.full(label.shape, tables[f, 0], jnp.float32) for f in range(4)]
    for zone in range(1, tables.shape[1]):
        here = label == float(zone)
        fields = [jnp.where(here, tables[f, zone], x) for f, x in enumerate(fields)]
    conduct[r, lo:hi] = fields[0]
    capacity[r, lo:hi] = fields[1]
    pre[r, lo:hi] = fields[2] * whole(2)
    act[r, lo:hi] = fields[3]
    dep[r, lo:hi] = whole(3)


def keeper(span, t, t_new, rims):
    lo, hi = span
    own = t.shape[0] - 2 * H

    def finish(r, update):
        value = (t[r, lo:hi] + update)[NEAR[0] - lo : NEAR[1] - lo]
        t_new[r, slice(*NEAR)] = value
        if rims is not None and r >= own:
            rims[0][r - own] = value
        if rims is not None and r < 2 * H:
            rims[1][r - H] = value

    return finish


def first_kernel(total_rows, scalars, reads, updates, makes, scratch):
    place, tables = scalars
    state, ub, rims = makes[:6], makes[6], makes[7:]
    matrix, held, (ua, cs, cd, uc), sems = scratch[0], scratch[1:5], scratch[5:9], scratch[9]
    t0, conduct, capacity, act, pre, dep = state
    work = ua, cs, cd, ub, uc
    rows = t0.shape[0]
    own = rows - 2 * H
    copies = [pltpu.make_async_copy(x, y, sems.at[i]) for i, (x, y) in enumerate(zip(reads, held))]
    for copy in copies:
        copy.start()
    suffix_matrix(matrix)
    tables_of = [{plane: i for i, plane in enumerate(planes(first, own))} for first in (True, False)]
    rim_planes = len(tables_of[0]) // 2

    def own_plane(r):
        def source(kind):
            for ref, table in zip(held, tables_of):
                if (kind, r) in table:
                    return ref, table[kind, r]

        return source

    def halo_plane(r):
        low = tables_of[0]

        def source(kind):
            if r < 0:
                at = low.get((kind, r + own))
                return None if at is None else (held[2], at - rim_planes)
            return (held[3], low[kind, r - own]) if (kind, r - own) in low else None

        return source

    copies[0].wait()
    copies[1].wait()
    for r in range(own):
        unpack_row(tables, own_plane(r), r + H, state)
    copies[2].wait()
    copies[3].wait()
    for r in range(H):
        unpack_row(tables, halo_plane(r - H), r, state)
        unpack_row(tables, halo_plane(own + r), own + r + H, state)
    lo, hi = WIDE

    def one(r):
        source, inverse, side, down = linearise(
            r, place[0] * own + r - H, total_rows, WIDE, t0, None, (conduct, capacity, act, pre), matrix
        )
        ua[r, lo:hi] = (source + dep[r, lo:hi]) * inverse
        cs[r, lo:hi] = side
        cd[r, lo:hi] = down

    over([(1, rows - 1)], one)
    sweeps(WIDE, work, [[(k, rows - k)] for k in (2, 3, 4)], keeper(WIDE, t0, ub, rims))


def later_kernel(outer, last, total_rows, scalars, reads, updates, makes, scratch):
    (place,) = scalars
    lo, hi = NEAR
    if outer:
        above, below, t0, conduct, capacity, act, pre, dep = reads[:8]
        t, ua, cs, cd, ub, uc = updates
        rims = None if last else makes
    else:
        t, t0, conduct, capacity, act, pre, dep = reads
        ua, cs, cd, ub, uc = makes[:5]
        rims = None
    rows = t0.shape[0]
    own = rows - 2 * H
    suffix_matrix(scratch[0])
    if outer:
        t[0:H, lo:hi] = above[...]
        t[H + own :, lo:hi] = below[...]

    def one(r):
        source, inverse, side, down = linearise(
            r, place[0] * own + r - H, total_rows, NEAR, t, t0, (conduct, capacity, act, pre), scratch[0]
        )
        ua[r, lo:hi] = (source + dep[r, lo:hi]) * inverse
        cs[r, lo:hi] = side
        cd[r, lo:hi] = down

    if last:
        out, blowing = makes[-2:]
        if outer:
            out[...], blowing[...] = reads[8][...], reads[9][...]
        core = slice(*CORE)
        mid = slice(CORE[0] - lo, CORE[1] - lo)

        def finish(r, update):
            value = t[r, core] + update[mid]
            out[:, r - H] = value.T.reshape(out.shape[0], 8, LANES)
            p = pre[r, core] * jnp.exp(act[r, core] * value / (1.0 + jnp.abs(value)))
            blowing[r - H : r - H + 1, :] = jnp.sum(p.T, axis=0, keepdims=True) * (1.0 / LANES)

    else:
        finish = keeper(NEAR, t, ub, rims)
    ranges = outer_rows if outer else inner_rows
    over(ranges(rows, 1), one)
    sweeps(NEAR, (ua, cs, cd, ub, uc), [ranges(rows, k) for k in (2, 3, 4)], finish)


def deliver_kernel(scalars, reads, updates, makes, scratch):
    (gathered,), (out,), (left, right) = reads, makes, scratch
    groups, rows3, _ = gathered.shape
    rows = rows3 // 3
    me = scalars[0][0]
    owners = gathered[:, 2 * rows :, :].astype(jnp.int32)
    shape = owners.shape
    number = lax.broadcasted_iota(jnp.int32, shape, 0) * rows + lax.broadcasted_iota(jnp.int32, shape, 1)
    first = jnp.min(jnp.where(owners == me, number, groups * rows))
    most = out.shape[0]
    first = jnp.minimum(first, groups * rows - most)
    high_of = lax.broadcasted_iota(jnp.int32, (most, LANES), 0)
    low_of = lax.broadcasted_iota(jnp.int32, (LANES, LANES), 0)
    for i in range(most):
        at = first + i
        group, r = at // rows, at % rows
        value = gathered[group, pl.ds(r, 1), :]
        slot = gathered[group, pl.ds(rows + r, 1), :].astype(jnp.int32)
        owner = gathered[group, pl.ds(2 * rows + r, 1), :].astype(jnp.int32)
        high = jnp.where(owner == me, slot >> 7, -1)
        low = slot & (LANES - 1)
        here = slice(LANES * i, LANES * (i + 1))
        hit = high_of == high
        for k, part in enumerate(split3(value)):
            left[most * k : most * (k + 1), here] = jnp.where(hit, part.astype(jnp.float32), 0.0).astype(
                jnp.bfloat16
            )
        right[:, here] = jnp.where(low_of == low, 1.0, 0.0).astype(jnp.bfloat16)
    parts = lax.dot_general(
        left[...], right[...], (((1,), (1,)), ((), ())), preferred_element_type=jnp.float32
    )
    out[...] = parts[:most] + parts[most : 2 * most] + parts[2 * most :]


def shards(
    kelvin_before_step,
    unburnt_resin_share,
    deposited_energy_amount,
    material_label,
    zonal_diffusivity,
    zonal_storage_coefficient,
    frequency_coefficient,
    arrhenius_barrier,
    stream_keeper,
    keeper_position,
):
    own, layers, columns = kelvin_before_step.shape
    n_axial, n_depth = lax.axis_size("axial"), lax.axis_size("depth")
    place = lax.axis_index("axial").astype(jnp.int32).reshape(1)
    total_rows = own * n_axial
    tables = jnp.stack(
        [zonal_diffusivity, zonal_storage_coefficient, frequency_coefficient, arrhenius_barrier]
    )
    rows = own + 2 * H
    extended = (rows, FULL, LANES)
    rim = (H, NEAR[1] - NEAR[0], LANES)
    matrix = [pltpu.VMEM((3 * LANES, LANES), jnp.bfloat16)]

    def up(x):
        return lax.ppermute(x, "axial", [(i, i + 1) for i in range(n_axial - 1)])

    def down(x):
        return lax.ppermute(x, "axial", [(i + 1, i) for i in range(n_axial - 1)])

    cells = [kelvin_before_step, material_label, unburnt_resin_share, deposited_energy_amount]
    cells = [kelvin_before_step, material_label, unburnt_resin_share, deposited_energy_amount]
    cells = [pltpu.with_memory_space_constraint(x, pltpu.HBM) for x in cells]

    def sent(first):
        return call(
            functools.partial(pack_kernel, first), "pack1" if first else "pack2", [], cells, [],
            [(n_depth, len(planes(first, own)), layers, LANES)],
            [pltpu.VMEM(x.shape, x.dtype) for x in cells]
            + [pltpu.VMEM((n_depth, len(planes(first, own)), layers, LANES), jnp.float32)]
            + [pltpu.SemaphoreType.DMA((4, 2)), pltpu.SemaphoreType.DMA((10,))],
            space=pltpu.HBM, out_space=pltpu.HBM,
        )[0]

    arrived = [lax.all_to_all(sent(first), "depth", 0, 0) for first in (True, False)]
    rims = (n_depth, len(planes(True, own)) // 2, layers, LANES)
    top, bottom = call(rims_kernel, "rims", [], arrived[:1], [], [rims] * 2, kept=False)
    came = [*arrived, up(top), down(bottom)]
    *arrays, top, bottom = call(
        functools.partial(first_kernel, total_rows), "newton1",
        [place, tables], [pltpu.with_memory_space_constraint(x, pltpu.HBM) for x in came], [],
        [extended] * 7 + [rim] * 2,
        matrix
        + [pltpu.VMEM(x.shape, jnp.float32) for x in came]
        + [pltpu.VMEM(extended, jnp.float32)] * 4
        + [pltpu.SemaphoreType.DMA((4,))],
        space=pltpu.HBM, limit=20,
    )
    t0, conduct, capacity, act, pre, dep = arrays[:6]
    t = arrays[6]
    for last in (False, True):
        above, below = up(top), down(bottom)
        fixed = [t0, conduct, capacity, act, pre, dep]
        results = [(n_depth, own, layers, LANES), (own, LANES)] if last else []
        work = call(
            functools.partial(later_kernel, False, last, total_rows), "newton3_inner" if last else "newton2_inner",
            [place], [t] + fixed, [], [extended] * 5 + results, matrix,
        )
        work = call(
            functools.partial(later_kernel, True, last, total_rows), "newton3_outer" if last else "newton2_outer",
            [place], [above, below] + fixed + work[5:], [t] + work[:5], results if last else [rim] * 2, matrix,
            kept=not last,
        )
        if not last:
            t, top, bottom = work[4], *work[6:]
    kelvin, blowing = work[6:]

    kelvin = lax.all_to_all(kelvin, "depth", 0, 0)
    kelvin = jnp.transpose(kelvin, (1, 2, 0, 3)).reshape(own, layers, columns)

    faces = jnp.concatenate(
        [blowing, keeper_position.astype(jnp.float32), stream_keeper.astype(jnp.float32)], axis=0
    )
    gathered = lax.all_gather(faces, "axial")
    slots = 2 * own * LANES
    (delivered,) = call(
        deliver_kernel, "deliver", [place], [gathered], [], [(slots // LANES, LANES)],
        [
            pltpu.VMEM((3 * slots // LANES, slots), jnp.bfloat16),
            pltpu.VMEM((LANES, slots), jnp.bfloat16),
        ],
        kept=False,
    )
    return (kelvin, delivered.reshape(slots))


def solution(mesh):
    cells = P("axial", "depth", None)
    faces = P("axial", "depth")
    return jax.shard_map(
        shards,
        mesh=mesh,
        in_specs=(cells, cells, cells, cells, P(), P(), P(), P(), faces, faces),
        out_specs=(cells, P(("axial", "depth"))),
        check_vma=False,
    )
```

```python
import functools

import jax
import jax.numpy as jnp
from jax import lax
from jax.experimental import pallas as pl
from jax.experimental.pallas import tpu as pltpu
from jax.sharding import PartitionSpec as P

SWEEPS = 4
H = 4
W = 12
EDGE = 16
LANES = 128
PAD = 8
SPAN = 2 * EDGE + LANES
FULL = SPAN + 2 * PAD
WIDE = (PAD, PAD + SPAN)
NEAR = (PAD + EDGE // 2, PAD + SPAN - EDGE // 2)
CORE = (PAD + EDGE, PAD + EDGE + LANES)
PACKED = 4 * H * 2 * W // LANES

VM = pl.BlockSpec(memory_space=pltpu.VMEM)
SM = pl.BlockSpec(memory_space=pltpu.SMEM)


def f32(*shape):
    return jax.ShapeDtypeStruct(shape, jnp.float32)


def call(kernel, name, scalars, reads, updates, makes, scratch=(), kept=True, space=pltpu.VMEM, out_space=pltpu.VMEM, limit=8):
    counts = [len(scalars), len(reads), len(updates), len(updates), len(makes), len(scratch)]

    def body(*refs):
        groups, at = [], 0
        for count in counts:
            groups.append(refs[at : at + count])
            at += count
        kernel(groups[0], groups[1], groups[3], groups[4], groups[5])

    first = len(scalars) + len(reads)
    results = pl.pallas_call(
        body,
        out_shape=[pltpu.VMEM(u.shape, jnp.float32) for u in updates]
        + [out_space(s, jnp.float32) if kept else f32(*s) for s in makes],
        in_specs=[SM] * len(scalars)
        + [pl.BlockSpec(memory_space=space)] * len(reads)
        + [VM] * len(updates),
        out_specs=[VM] * len(updates) + [pl.BlockSpec(memory_space=out_space)] * len(makes),
        input_output_aliases={first + i: i for i in range(len(updates))},
        scratch_shapes=list(scratch),
        compiler_params=pltpu.CompilerParams(vmem_limit_bytes=limit * 1024 * 1024),
        name=name,
    )(*scalars, *reads, *updates)
    return list(results)


def lane_iota(rows):
    return lax.broadcasted_iota(jnp.int32, (rows, LANES), 1)


def split3(x):
    a = x.astype(jnp.bfloat16)
    rest = x - a.astype(jnp.float32)
    b = rest.astype(jnp.bfloat16)
    c = (rest - b.astype(jnp.float32)).astype(jnp.bfloat16)
    return a, b, c


def over(ranges, body):
    for low, high in ranges:
        for r in range(low, high):
            body(r)


def groups(first, own):
    return [0, own - H] if first else list(range(H, own - H, H))


def planes(first, own):
    result = []
    for g in groups(first, own):
        result += [(k, g + i) for k in range(4) for i in range(H)]
        result += [(4, (g, j)) for j in range(PACKED)]
    return result


GROUP = 4 * H + PACKED


def rim_planes(side):
    fixed = range(1, H) if side else range(H - 1)
    return list(range(H)) + [k * H + i for k in range(1, 4) for i in fixed] + list(range(4 * H, GROUP))


def pack_kernel(first, scalars, ins, updates, makes, scratch):
    (result,), held, out, sems, out_sems = makes, scratch[:4], scratch[4], scratch[5], scratch[6]
    slices = out.shape[0]
    own = ins[0].shape[0]
    lane = lane_iota(8)
    bands = [slice(0, H), slice(own - H, own)] if first else [slice(H, own - H)]
    copies = [
        pltpu.make_async_copy(x.at[band], y.at[band], sems.at[i, j])
        for i, (x, y) in enumerate(zip(ins, held))
        for j, band in enumerate(bands)
    ]
    for copy in copies:
        copy.start()
    for copy in copies:
        copy.wait()

    def tile(k, a, s):
        return held[k][a, :, LANES * s : LANES * (s + 1)].astype(jnp.float32)

    sent = []
    order = planes(first, own)
    for p, (kind, a) in enumerate(order):
        if kind < 4:
            for s in range(slices):
                out[s, p] = tile(kind, a, s)
        else:
            (g, part), place = a, a[1] * LANES
            pieces = range(place // (2 * W), (place + LANES - 1) // (2 * W) + 1)
            turned = {
                m: [pltpu.roll(tile(m % 4, g + m // 4, s), (2 * W * m + W) % LANES, 1) for s in range(slices)]
                for m in pieces
            }
            for s in range(slices):
                value = None
                for m in pieces:
                    for start, piece in (
                        (2 * W * m, turned[m][s - 1]),
                        (2 * W * m + W, turned[m][(s + 1) % slices]),
                    ):
                        value = piece if start <= place else jnp.where(lane >= start - place, piece, value)
                out[s, p] = value
        if (p + 1) % GROUP in (0, 2 * H):
            band = slice(sent[-1][1] if sent else 0, p + 1)
            copy = pltpu.make_async_copy(out.at[:, band], result.at[:, band], out_sems.at[len(sent)])
            copy.start()
            sent.append((copy, p + 1))
    for copy, _ in sent:
        copy.wait()


def rims_kernel(scalars, reads, updates, makes, scratch):
    (arrived,), (top, bottom) = reads, makes
    for side, ref in enumerate((bottom, top)):
        for p, plane in enumerate(rim_planes(side)):
            ref[:, p] = arrived[:, side * GROUP + plane]


def suffix_matrix(m_ref):
    rows, cols = m_ref.shape
    source = lax.broadcasted_iota(jnp.int32, (rows, cols), 0) & (LANES - 1)
    target = lax.broadcasted_iota(jnp.int32, (rows, cols), 1)
    m_ref[...] = jnp.where(source > target, 4.0 / LANES, 0.0).astype(jnp.bfloat16)


def linearise(r, row, total_rows, span, t, t0, fields, m_ref):
    lo, hi = span
    conduct, capacity, act, pre = fields
    lane = lane_iota(hi - lo)
    tc = t[r, lo:hi]
    a = act[r, lo:hi]
    q = 1.0 / (1.0 + jnp.abs(tc))
    aq = a * q
    p = pre[r, lo:hi] * jnp.exp(aq * tc)
    gas = jnp.dot(jnp.concatenate(split3(p), axis=1), m_ref[...], preferred_element_type=jnp.float32)
    c = conduct[r, lo:hi]
    cap = capacity[r, lo:hi]
    deeper = jnp.where(lane == LANES - 1, 0.0, pltpu.roll(tc, LANES - 1, 1))
    shallower = jnp.where(lane == 0, 0.0, pltpu.roll(tc, 1, 1))
    pairs = t[r - 1, lo:hi] + t[r + 1, lo:hi] + t[r, lo - 1 : hi - 1] + t[r, lo + 1 : hi + 1]
    spread = pairs + 2.0 * (deeper + shallower) - 8.0 * tc
    source = c * spread - 0.5 * p - gas * (tc - deeper)
    if t0 is not None:
        source = source - cap * (tc - t0[r, lo:hi])
    diagonal = cap + 8.0 * c + 0.5 * p * (aq * q) + gas
    inside = jnp.where((row >= 0) & (row < total_rows), 1.0, 0.0)
    inverse = inside / diagonal
    return source, inverse, c * inverse, jnp.where(lane == LANES - 1, 0.0, (2.0 * c + gas) * inverse)


CHUNK = 80


def chunks(span):
    lo, hi = span
    return [(c, min(c + CHUNK, hi)) for c in range(lo, hi, CHUNK)]


def sweeps(span, work, ranges, finish):
    first, side, down, b, c = work

    def swept(src, r, lo, hi):
        lane = lane_iota(hi - lo)
        u = src[r, lo:hi]
        pairs = src[r - 1, lo:hi] + src[r + 1, lo:hi] + src[r, lo - 1 : hi - 1] + src[r, lo + 1 : hi + 1]
        shallower = jnp.where(lane == 0, 0.0, pltpu.roll(u, 1, 1))
        deeper = pltpu.roll(u, LANES - 1, 1)
        return first[r, lo:hi] + side[r, lo:hi] * (pairs + 2.0 * shallower) + down[r, lo:hi] * deeper

    def second(r):
        for lo, hi in chunks(span):
            b[r, lo:hi] = swept(first, r, lo, hi)

    def third(r):
        for lo, hi in chunks(span):
            c[r, lo:hi] = swept(b, r, lo, hi)

    def last(r):
        finish(r, lambda lo, hi: swept(c, r, lo, hi))

    over(ranges[0], second)
    over(ranges[1], third)
    over(ranges[2], last)


def inner_rows(rows, k):
    return [(H + k, rows - H - k)]


def outer_rows(rows, k):
    return [(k, H + k), (rows - H - k, rows - k)]


def from_cells(ref, r):
    x = ref[:, r]
    return x.reshape(x.shape[0] * x.shape[1], LANES).T


def unpack_rows(ref, plane_of, first, lo, arrays):
    edges = jnp.concatenate([from_cells(ref, plane_of(4 * H + j)) for j in range(PACKED)], axis=0)
    pad = EDGE - W
    for i in range(H):
        for kind, array in enumerate(arrays):
            plane = plane_of(kind * H + i)
            if plane is None:
                continue
            at = 2 * W * (4 * i + kind)
            array[first + i, lo : lo + EDGE] = pltpu.roll(edges[at : at + EDGE], pad, 0)
            array[first + i, lo + EDGE : lo + EDGE + LANES] = from_cells(ref, plane)
            array[first + i, lo + EDGE + LANES : lo + SPAN] = pltpu.roll(edges[at + 2 * W - EDGE : at + 2 * W], EDGE - pad, 0)


def look_up(tables, r, state):
    _, conduct, capacity, act, pre, _ = state
    wide = slice(*WIDE)
    label = conduct[r, wide]
    fields = [jnp.full(label.shape, tables[f, 0], jnp.float32) for f in range(4)]
    for zone in range(1, tables.shape[1]):
        here = label == float(zone)
        fields = [jnp.where(here, tables[f, zone], x) for f, x in enumerate(fields)]
    conduct[r, wide] = fields[0]
    capacity[r, wide] = fields[1]
    pre[r, wide] = fields[2] * pre[r, wide]
    act[r, wide] = fields[3]


def keeper(t, t_new):
    def finish(r, update):
        for lo, hi in chunks(NEAR):
            t_new[r, lo:hi] = t[r, lo:hi] + update(lo, hi)

    return finish


def hand_on(t_new, rims):
    own = t_new.shape[0] - 2 * H
    rims[0][...] = t_new[own : own + H, slice(*NEAR)]
    rims[1][...] = t_new[H : 2 * H, slice(*NEAR)]


def rims_in_kernel(scalars, reads, updates, makes, scratch):
    arrived, above, below = reads
    arrays, sems = scratch[:4], scratch[4]
    copies = []

    def rim(side):
        table = {plane: p for p, plane in enumerate(rim_planes(side))}
        return table.get

    def send(half):
        rows = slice(half * 2 * H, (half + 1) * 2 * H)
        for i, (x, y) in enumerate(zip(arrays, makes)):
            copies.append(pltpu.make_async_copy(x.at[rows], y.at[rows], sems.at[i, half]))
            copies[-1].start()

    unpack_rows(above, rim(1), 0, 0, arrays)
    unpack_rows(arrived, lambda plane: plane, H, 0, arrays)
    send(0)
    unpack_rows(arrived, lambda plane: GROUP + plane, 2 * H, 0, arrays)
    unpack_rows(below, rim(0), 3 * H, 0, arrays)
    send(1)
    for copy in copies:
        copy.wait()


def first_kernel(total_rows, scalars, reads, updates, makes, scratch):
    place, tables = scalars
    arrived, rims_in = reads[0], reads[1:]
    state, (ub, *rims) = makes[:6], makes[6:]
    matrix, held, (ua, cs, cd, uc), sem, sems = scratch[0], scratch[1], scratch[2:6], scratch[6], scratch[7]
    t0, conduct, capacity, act, pre, dep = state
    raw = t0, conduct, pre, dep
    work = ua, cs, cd, ub, uc
    rows = t0.shape[0]
    own = rows - 2 * H
    lo, hi = WIDE
    firsts = groups(False, own)
    mine = []
    for i in range(len(firsts)):
        band = slice(i * GROUP, (i + 1) * GROUP)
        mine.append(pltpu.make_async_copy(arrived.at[:, band], held.at[:, band], sem.at[i]))
    others = [
        pltpu.make_async_copy(
            x.at[half * 2 * H : (half + 1) * 2 * H], y.at[first : first + 2 * H, lo:hi], sems.at[i, half]
        )
        for half, first in enumerate((0, own))
        for i, (x, y) in enumerate(zip(rims_in, raw))
    ]
    for copy in mine:
        copy.start()
    suffix_matrix(matrix)

    def one(r):
        for lo, hi in chunks(WIDE):
            source, inverse, side, down = linearise(
                r, place[0] * own + r - H, total_rows, (lo, hi), t0, None, (conduct, capacity, act, pre), matrix
            )
            ua[r, lo:hi] = (source + dep[r, lo:hi]) * inverse
            cs[r, lo:hi] = side
            cd[r, lo:hi] = down

    for i, g in enumerate(firsts):
        mine[i].wait()
        if i == 0:
            for copy in others:
                copy.start()
        unpack_rows(held, lambda plane: i * GROUP + plane, g + H, WIDE[0], raw)
        for r in range(g + H, g + 2 * H):
            look_up(tables, r, state)
    inner = 2 * H + 1, own - 1
    over([inner], one)
    for copy in others:
        copy.wait()
    for r in [*range(1, 2 * H), *range(own, rows - 1)]:
        look_up(tables, r, state)
    over([(1, inner[0]), (inner[1], rows - 1)], one)
    sweeps(WIDE, work, [[(k, rows - k)] for k in (2, 3, 4)], keeper(t0, ub))
    hand_on(ub, rims)


def later_kernel(outer, last, total_rows, scalars, reads, updates, makes, scratch):
    (place,) = scalars
    lo, hi = NEAR
    if outer:
        above, below, t0, conduct, capacity, act, pre, dep = reads[:8]
        t, ua, cs, cd, ub, uc = updates
        rims = None if last else makes
    else:
        t, t0, conduct, capacity, act, pre, dep = reads
        ua, cs, cd, ub, uc = makes[:5]
        rims = None
    rows = t0.shape[0]
    own = rows - 2 * H
    suffix_matrix(scratch[0])
    if outer:
        t[0:H, lo:hi] = above[...]
        t[H + own :, lo:hi] = below[...]

    def one(r):
        for lo, hi in chunks(NEAR):
            source, inverse, side, down = linearise(
                r, place[0] * own + r - H, total_rows, (lo, hi), t, t0, (conduct, capacity, act, pre), scratch[0]
            )
            ua[r, lo:hi] = (source + dep[r, lo:hi]) * inverse
            cs[r, lo:hi] = side
            cd[r, lo:hi] = down

    if last:
        out, blowing = makes[-2:]
        if outer:
            out[...], blowing[...] = reads[8][...], reads[9][...]
        core = slice(*CORE)

        def finish(r, update):
            value = t[r, core] + update(*CORE)
            out[:, r - H] = value.T.reshape(out.shape[0], 8, LANES)
            p = pre[r, core] * jnp.exp(act[r, core] * value / (1.0 + jnp.abs(value)))
            blowing[pl.ds(r - H, 1), :] = jnp.sum(p.T, axis=0, keepdims=True) * (1.0 / LANES)

    else:
        finish = keeper(t, ub)
    ranges = outer_rows if outer else inner_rows
    over(ranges(rows, 1), one)
    sweeps(NEAR, (ua, cs, cd, ub, uc), [ranges(rows, k) for k in (2, 3, 4)], finish)
    if outer and not last:
        hand_on(ub, rims)


def deliver_kernel(scalars, reads, updates, makes, scratch):
    gathered, arrived = reads
    (out, kelvin), (left, right, sems) = makes, scratch
    copies = [
        pltpu.make_async_copy(arrived.at[s], kelvin.at[:, :, LANES * s : LANES * (s + 1)], sems.at[s])
        for s in range(arrived.shape[0])
    ]
    for copy in copies:
        copy.start()
    groups, rows3, _ = gathered.shape
    rows = rows3 // 3
    me = scalars[0][0]
    owners = gathered[:, 2 * rows :, :].astype(jnp.int32)
    shape = owners.shape
    number = lax.broadcasted_iota(jnp.int32, shape, 0) * rows + lax.broadcasted_iota(jnp.int32, shape, 1)
    first = jnp.min(jnp.where(owners == me, number, groups * rows))
    most = out.shape[0]
    first = jnp.minimum(first, groups * rows - most)
    high_of = lax.broadcasted_iota(jnp.int32, (most, LANES), 0)
    low_of = lax.broadcasted_iota(jnp.int32, (LANES, LANES), 0)
    for i in range(most):
        at = first + i
        group, r = at // rows, at % rows
        value = gathered[group, pl.ds(r, 1), :]
        slot = gathered[group, pl.ds(rows + r, 1), :].astype(jnp.int32)
        owner = gathered[group, pl.ds(2 * rows + r, 1), :].astype(jnp.int32)
        high = jnp.where(owner == me, slot >> 7, -1)
        low = slot & (LANES - 1)
        here = slice(LANES * i, LANES * (i + 1))
        hit = high_of == high
        for k, part in enumerate(split3(value)):
            left[most * k : most * (k + 1), here] = jnp.where(hit, part.astype(jnp.float32), 0.0).astype(
                jnp.bfloat16
            )
        right[:, here] = jnp.where(low_of == low, 1.0, 0.0).astype(jnp.bfloat16)
    parts = lax.dot_general(
        left[...], right[...], (((1,), (1,)), ((), ())), preferred_element_type=jnp.float32
    )
    out[...] = parts[:most] + parts[most : 2 * most] + parts[2 * most :]
    for copy in copies:
        copy.wait()


def shards(
    kelvin_before_step,
    unburnt_resin_share,
    deposited_energy_amount,
    material_label,
    zonal_diffusivity,
    zonal_storage_coefficient,
    frequency_coefficient,
    arrhenius_barrier,
    stream_keeper,
    keeper_position,
):
    own, layers, columns = kelvin_before_step.shape
    n_axial, n_depth = lax.axis_size("axial"), lax.axis_size("depth")
    place = lax.axis_index("axial").astype(jnp.int32).reshape(1)
    total_rows = own * n_axial
    tables = jnp.stack(
        [zonal_diffusivity, zonal_storage_coefficient, frequency_coefficient, arrhenius_barrier]
    )
    rows = own + 2 * H
    extended = (rows, FULL, LANES)
    rim = (H, NEAR[1] - NEAR[0], LANES)
    matrix = [pltpu.VMEM((3 * LANES, LANES), jnp.bfloat16)]

    def up(x):
        return lax.ppermute(x, "axial", [(i, i + 1) for i in range(n_axial - 1)])

    def down(x):
        return lax.ppermute(x, "axial", [(i + 1, i) for i in range(n_axial - 1)])

    cells = [kelvin_before_step, material_label, unburnt_resin_share, deposited_energy_amount]
    cells = [kelvin_before_step, material_label, unburnt_resin_share, deposited_energy_amount]
    cells = [pltpu.with_memory_space_constraint(x, pltpu.HBM) for x in cells]

    def sent(first):
        return call(
            functools.partial(pack_kernel, first), "pack1" if first else "pack2", [], cells, [],
            [(n_depth, len(planes(first, own)), layers, LANES)],
            [pltpu.VMEM(x.shape, x.dtype) for x in cells]
            + [pltpu.VMEM((n_depth, len(planes(first, own)), layers, LANES), jnp.float32)]
            + [pltpu.SemaphoreType.DMA((4, 2)), pltpu.SemaphoreType.DMA((10,))],
            space=pltpu.HBM, out_space=pltpu.HBM,
        )[0]

    arrived = [lax.all_to_all(sent(first), "depth", 0, 0) for first in (True, False)]
    rims = [(n_depth, len(rim_planes(side)), layers, LANES) for side in (1, 0)]
    top, bottom = call(rims_kernel, "rims", [], arrived[:1], [], rims, kept=False)
    outer = (4 * H, SPAN, LANES)
    came = call(
        rims_in_kernel, "rims_in", [], [arrived[0], up(top), down(bottom)], [], [outer] * 4,
        [pltpu.VMEM(outer, jnp.float32)] * 4 + [pltpu.SemaphoreType.DMA((4, 2))],
        out_space=pltpu.HBM, limit=16,
    )
    came = [pltpu.with_memory_space_constraint(x, pltpu.HBM) for x in [arrived[1], *came]]
    *arrays, top, bottom = call(
        functools.partial(first_kernel, total_rows), "newton1",
        [place, tables], came, [], [extended] * 7 + [rim] * 2,
        matrix
        + [pltpu.VMEM(came[0].shape, jnp.float32)]
        + [pltpu.VMEM(extended, jnp.float32)] * 4
        + [pltpu.SemaphoreType.DMA((2,)), pltpu.SemaphoreType.DMA((4, 2))],
        space=pltpu.HBM, limit=14,
    )
    t0, conduct, capacity, act, pre, dep = arrays[:6]
    t = arrays[6]
    for last in (False, True):
        above, below = up(top), down(bottom)
        fixed = [t0, conduct, capacity, act, pre, dep]
        results = [(n_depth, own, layers, LANES), (own, LANES)] if last else []
        work = call(
            functools.partial(later_kernel, False, last, total_rows), "newton3_inner" if last else "newton2_inner",
            [place], [t] + fixed, [], [extended] * 5 + results, matrix,
        )
        work = call(
            functools.partial(later_kernel, True, last, total_rows), "newton3_outer" if last else "newton2_outer",
            [place], [above, below] + fixed + work[5:], [t] + work[:5], results if last else [rim] * 2, matrix,
            kept=not last,
        )
        if not last:
            t, top, bottom = work[4], *work[6:]
    kelvin, blowing = work[6:]

    kelvin = lax.all_to_all(kelvin, "depth", 0, 0)

    faces = jnp.concatenate(
        [blowing, keeper_position.astype(jnp.float32), stream_keeper.astype(jnp.float32)], axis=0
    )
    gathered = lax.all_gather(faces, "axial")
    slots = 2 * own * LANES
    any_space = pl.BlockSpec(memory_space=pl.ANY)
    delivered, kelvin = pl.pallas_call(
        lambda place, *refs: deliver_kernel([place], refs[:2], [], refs[2:4], refs[4:]),
        out_shape=[f32(slots // LANES, LANES), f32(own, layers, columns)],
        in_specs=[SM, VM, any_space],
        out_specs=[VM, any_space],
        scratch_shapes=[
            pltpu.VMEM((3 * slots // LANES, slots), jnp.bfloat16),
            pltpu.VMEM((LANES, slots), jnp.bfloat16),
            pltpu.SemaphoreType.DMA((n_depth,)),
        ],
        compiler_params=pltpu.CompilerParams(vmem_limit_bytes=8 * 1024 * 1024),
        name="deliver",
    )(place, gathered, kelvin)
    return (kelvin, delivered.reshape(slots))


def solution(mesh):
    cells = P("axial", "depth", None)
    faces = P("axial", "depth")
    return jax.shard_map(
        shards,
        mesh=mesh,
        in_specs=(cells, cells, cells, cells, P(), P(), P(), P(), faces, faces),
        out_specs=(cells, P(("axial", "depth"))),
        check_vma=False,
    )
```

```python
import functools

import jax
import jax.numpy as jnp
from jax import lax
from jax.experimental import pallas as pl
from jax.experimental.pallas import tpu as pltpu
from jax.sharding import PartitionSpec as P

SWEEPS = 4
H = 4
W = 12
EDGE = 16
LANES = 128
PAD = 8
SPAN = 2 * EDGE + LANES
FULL = SPAN + 2 * PAD
WIDE = (PAD, PAD + SPAN)
NEAR = (PAD + EDGE // 2, PAD + SPAN - EDGE // 2)
CORE = (PAD + EDGE, PAD + EDGE + LANES)
PACKED = 4 * H * 2 * W // LANES

VM = pl.BlockSpec(memory_space=pltpu.VMEM)
SM = pl.BlockSpec(memory_space=pltpu.SMEM)


def f32(*shape):
    return jax.ShapeDtypeStruct(shape, jnp.float32)


def call(kernel, name, scalars, reads, updates, makes, scratch=(), kept=True, space=pltpu.VMEM, out_space=pltpu.VMEM, limit=8):
    counts = [len(scalars), len(reads), len(updates), len(updates), len(makes), len(scratch)]

    def body(*refs):
        groups, at = [], 0
        for count in counts:
            groups.append(refs[at : at + count])
            at += count
        kernel(groups[0], groups[1], groups[3], groups[4], groups[5])

    first = len(scalars) + len(reads)
    results = pl.pallas_call(
        body,
        out_shape=[pltpu.VMEM(u.shape, jnp.float32) for u in updates]
        + [out_space(s, jnp.float32) if kept else f32(*s) for s in makes],
        in_specs=[SM] * len(scalars)
        + [pl.BlockSpec(memory_space=space)] * len(reads)
        + [VM] * len(updates),
        out_specs=[VM] * len(updates) + [pl.BlockSpec(memory_space=out_space)] * len(makes),
        input_output_aliases={first + i: i for i in range(len(updates))},
        scratch_shapes=list(scratch),
        compiler_params=pltpu.CompilerParams(vmem_limit_bytes=limit * 1024 * 1024),
        name=name,
    )(*scalars, *reads, *updates)
    return list(results)


def lane_iota(rows):
    return lax.broadcasted_iota(jnp.int32, (rows, LANES), 1)


def split3(x):
    a = x.astype(jnp.bfloat16)
    rest = x - a.astype(jnp.float32)
    b = rest.astype(jnp.bfloat16)
    c = (rest - b.astype(jnp.float32)).astype(jnp.bfloat16)
    return a, b, c


def over(ranges, body):
    for low, high in ranges:
        for r in range(low, high):
            body(r)


def groups(first, own):
    return [0, own - H] if first else list(range(H, own - H, H))


def planes(first, own):
    result = []
    for g in groups(first, own):
        result += [(k, g + i) for k in range(4) for i in range(H)]
        result += [(4, (g, j)) for j in range(PACKED)]
    return result


GROUP = 4 * H + PACKED


def rim_planes(side):
    fixed = range(1, H) if side else range(H - 1)
    return list(range(H)) + [k * H + i for k in range(1, 4) for i in fixed] + list(range(4 * H, GROUP))


def pack_kernel(first, scalars, ins, updates, makes, scratch):
    (result,), held, out, sems, out_sems = makes, scratch[:4], scratch[4], scratch[5], scratch[6]
    slices = out.shape[0]
    own = ins[0].shape[0]
    lane = lane_iota(8)
    bands = [slice(0, H), slice(own - H, own)] if first else [slice(H, own - H)]
    copies = {
        (i, j): pltpu.make_async_copy(x.at[band], y.at[band], sems.at[i, j])
        for j, band in enumerate(bands)
        for i, (x, y) in enumerate(zip(ins, held))
    }
    for copy in copies.values():
        copy.start()

    def tile(k, a, s):
        return held[k][a, :, LANES * s : LANES * (s + 1)].astype(jnp.float32)

    sent = []
    order = planes(first, own)
    for p, (kind, a) in enumerate(order):
        if kind < 4:
            band = min(p // GROUP, len(bands) - 1)
            if (kind, band) in copies:
                copies.pop((kind, band)).wait()
            for s in range(slices):
                out[s, p] = tile(kind, a, s)
        else:
            (g, part), place = a, a[1] * LANES
            pieces = range(place // (2 * W), (place + LANES - 1) // (2 * W) + 1)
            turned = {
                m: [pltpu.roll(tile(m % 4, g + m // 4, s), (2 * W * m + W) % LANES, 1) for s in range(slices)]
                for m in pieces
            }
            for s in range(slices):
                value = None
                for m in pieces:
                    for start, piece in (
                        (2 * W * m, turned[m][s - 1]),
                        (2 * W * m + W, turned[m][(s + 1) % slices]),
                    ):
                        value = piece if start <= place else jnp.where(lane >= start - place, piece, value)
                out[s, p] = value
        if (p + 1) % GROUP in (0, 2 * H):
            band = slice(sent[-1][1] if sent else 0, p + 1)
            copy = pltpu.make_async_copy(out.at[:, band], result.at[:, band], out_sems.at[len(sent)])
            copy.start()
            sent.append((copy, p + 1))
    for copy, _ in sent:
        copy.wait()


def rims_kernel(scalars, reads, updates, makes, scratch):
    (arrived,), (top, bottom) = reads, makes
    for side, ref in enumerate((bottom, top)):
        for p, plane in enumerate(rim_planes(side)):
            ref[:, p] = arrived[:, side * GROUP + plane]


def suffix_matrix(m_ref):
    rows, cols = m_ref.shape
    source = lax.broadcasted_iota(jnp.int32, (rows, cols), 0) & (LANES - 1)
    target = lax.broadcasted_iota(jnp.int32, (rows, cols), 1)
    m_ref[...] = jnp.where(source > target, 4.0 / LANES, 0.0).astype(jnp.bfloat16)


def linearise(r, row, total_rows, span, t, t0, fields, m_ref):
    lo, hi = span
    conduct, capacity, act, pre = fields
    lane = lane_iota(hi - lo)
    tc = t[r, lo:hi]
    a = act[r, lo:hi]
    q = 1.0 / (1.0 + jnp.abs(tc))
    aq = a * q
    p = pre[r, lo:hi] * jnp.exp(aq * tc)
    gas = jnp.dot(jnp.concatenate(split3(p), axis=1), m_ref[...], preferred_element_type=jnp.float32)
    c = conduct[r, lo:hi]
    cap = capacity[r, lo:hi]
    deeper = jnp.where(lane == LANES - 1, 0.0, pltpu.roll(tc, LANES - 1, 1))
    shallower = jnp.where(lane == 0, 0.0, pltpu.roll(tc, 1, 1))
    pairs = t[r - 1, lo:hi] + t[r + 1, lo:hi] + t[r, lo - 1 : hi - 1] + t[r, lo + 1 : hi + 1]
    spread = pairs + 2.0 * (deeper + shallower) - 8.0 * tc
    source = c * spread - 0.5 * p - gas * (tc - deeper)
    if t0 is not None:
        source = source - cap * (tc - t0[r, lo:hi])
    diagonal = cap + 8.0 * c + 0.5 * p * (aq * q) + gas
    inside = jnp.where((row >= 0) & (row < total_rows), 1.0, 0.0)
    inverse = inside / diagonal
    return source, inverse, c * inverse, jnp.where(lane == LANES - 1, 0.0, (2.0 * c + gas) * inverse)


CHUNK = 80


def chunks(span):
    lo, hi = span
    return [(c, min(c + CHUNK, hi)) for c in range(lo, hi, CHUNK)]


def sweeps(span, work, ranges, finish):
    first, side, down, b, c = work

    def swept(src, r, lo, hi):
        lane = lane_iota(hi - lo)
        u = src[r, lo:hi]
        pairs = src[r - 1, lo:hi] + src[r + 1, lo:hi] + src[r, lo - 1 : hi - 1] + src[r, lo + 1 : hi + 1]
        shallower = jnp.where(lane == 0, 0.0, pltpu.roll(u, 1, 1))
        deeper = pltpu.roll(u, LANES - 1, 1)
        return first[r, lo:hi] + side[r, lo:hi] * (pairs + 2.0 * shallower) + down[r, lo:hi] * deeper

    def second(r):
        for lo, hi in chunks(span):
            b[r, lo:hi] = swept(first, r, lo, hi)

    def third(r):
        for lo, hi in chunks(span):
            c[r, lo:hi] = swept(b, r, lo, hi)

    def last(r):
        finish(r, lambda lo, hi: swept(c, r, lo, hi))

    over(ranges[0], second)
    over(ranges[1], third)
    over(ranges[2], last)


def inner_rows(rows, k):
    return [(H + k, rows - H - k)]


def outer_rows(rows, k):
    return [(k, H + k), (rows - H - k, rows - k)]


def from_cells(ref, r):
    x = ref[:, r]
    return x.reshape(x.shape[0] * x.shape[1], LANES).T


def unpack_rows(ref, plane_of, first, lo, arrays):
    edges = jnp.concatenate([from_cells(ref, plane_of(4 * H + j)) for j in range(PACKED)], axis=0)
    pad = EDGE - W
    for i in range(H):
        for kind, array in enumerate(arrays):
            plane = plane_of(kind * H + i)
            if plane is None:
                continue
            at = 2 * W * (4 * i + kind)
            array[first + i, lo : lo + EDGE] = pltpu.roll(edges[at : at + EDGE], pad, 0)
            array[first + i, lo + EDGE : lo + EDGE + LANES] = from_cells(ref, plane)
            array[first + i, lo + EDGE + LANES : lo + SPAN] = pltpu.roll(edges[at + 2 * W - EDGE : at + 2 * W], EDGE - pad, 0)


def look_up(tables, r, wide, state):
    _, conduct, capacity, act, pre, _ = state
    label = conduct[r, wide]
    fields = [jnp.full(label.shape, tables[f, 0], jnp.float32) for f in range(4)]
    for zone in range(1, tables.shape[1]):
        here = label == float(zone)
        fields = [jnp.where(here, tables[f, zone], x) for f, x in enumerate(fields)]
    conduct[r, wide] = fields[0]
    capacity[r, wide] = fields[1]
    pre[r, wide] = fields[2] * pre[r, wide]
    act[r, wide] = fields[3]


def keeper(t, t_new):
    def finish(r, update):
        for lo, hi in chunks(NEAR):
            t_new[r, lo:hi] = t[r, lo:hi] + update(lo, hi)

    return finish


def hand_on(t_new, rims):
    own = t_new.shape[0] - 2 * H
    rims[0][...] = t_new[own : own + H, slice(*NEAR)]
    rims[1][...] = t_new[H : 2 * H, slice(*NEAR)]


def unpack_own_kernel(scalars, reads, updates, makes, scratch):
    t0, conduct, capacity, act, pre, dep = makes
    for half in range(2):
        unpack_rows(reads[0], lambda plane: half * GROUP + plane, half * H, 0, (t0, conduct, pre, dep))
    for r in range(2 * H):
        look_up(scalars[0], r, slice(0, SPAN), makes)


def outer_kernel(total_rows, own, scalars, reads, updates, makes, scratch):
    place, tables = scalars
    above, below, own_rims = reads[0], reads[1], reads[2:]
    arrays, matrix, sems = scratch[:9], scratch[9], scratch[10]
    state, work = arrays[:6], arrays[6:]
    t0, conduct, capacity, act, pre, dep = state
    lo, hi = WIDE
    copies = []

    def send(which):
        for i in which:
            copies.append(pltpu.make_async_copy(arrays[i].at[:, lo:hi], makes[i], sems.at[i]))
            copies[-1].start()

    def rim(side):
        table = {plane: p for p, plane in enumerate(rim_planes(side))}
        return table.get

    suffix_matrix(matrix)
    for x, y in zip(own_rims, state):
        y[H : 3 * H, lo:hi] = x[...]
    unpack_rows(above, rim(1), 0, lo, (t0, conduct, pre, dep))
    unpack_rows(below, rim(0), 3 * H, lo, (t0, conduct, pre, dep))
    send([0, 5])
    for r in [*range(1, H), *range(3 * H, 4 * H - 1)]:
        look_up(tables, r, slice(lo, hi), state)
    send([1, 2, 3, 4])
    for first, shift in ((1, -H), (2 * H + 1, own - 3 * H)):
        one = first_row(total_rows, place, own, shift, state, work, matrix)
        over([(first, first + 2 * H - 2)], one)
    send([6, 7, 8])
    for copy in copies:
        copy.wait()


def first_kernel(total_rows, scalars, reads, updates, makes, scratch):
    place, tables = scalars
    arrived, came = reads[0], reads[1:]
    state, work, rims = makes[:6], makes[6:11], makes[11:]
    matrix, held, sem, sems = scratch
    t0, conduct, capacity, act, pre, dep = state
    ua, cs, cd, ub, uc = work
    rows = t0.shape[0]
    own = rows - 2 * H
    lo, hi = WIDE
    firsts = groups(False, own)
    mine = []
    for i in range(len(firsts)):
        band = slice(i * GROUP, (i + 1) * GROUP)
        mine.append(pltpu.make_async_copy(arrived.at[:, band], held.at[:, band], sem.at[i]))
    others = []
    for i, (x, y) in enumerate(zip(came, (*state, ua, cs, cd))):
        edge = 0 if i < 6 else 1
        for half, shift in enumerate((0, own - 2 * H)):
            low, high = half * 2 * H + edge, (half + 1) * 2 * H - edge
            others.append(
                pltpu.make_async_copy(x.at[low:high], y.at[low + shift : high + shift, lo:hi], sems.at[i, half])
            )
    for copy in mine:
        copy.start()
    suffix_matrix(matrix)

    for i, g in enumerate(firsts):
        mine[i].wait()
        if i == 0:
            for copy in others:
                copy.start()
        unpack_rows(held, lambda plane: i * GROUP + plane, g + H, lo, (t0, conduct, pre, dep))
        for r in range(g + H, g + 2 * H):
            look_up(tables, r, slice(lo, hi), state)
    one = first_row(total_rows, place, own, -H, state, work, matrix)
    middle = rows // 2 - 1, rows // 2 + 1
    over([(2 * H + 1, middle[0]), (middle[1], own - 1)], one)
    for copy in others[:12]:
        copy.wait()
    over([(2 * H - 1, 2 * H + 1), (own - 1, own + 1)], one)
    for copy in others[12:]:
        copy.wait()
    sweeps(WIDE, work, [rim_rows(rows, k) for k in (2, 3, 4)], keeper(t0, ub))
    hand_on(ub, rims)


def rim_rows(rows, k):
    return [(k, 3 * H - k), (rows - 3 * H + k, rows - k)]


def rest_rows(rows, k):
    return [(3 * H - k, rows - 3 * H + k)]


def first_row(total_rows, place, own, shift, state, work, matrix):
    t0, conduct, capacity, act, pre, dep = state
    ua, cs, cd = work[:3]

    def one(r):
        for lo, hi in chunks(WIDE):
            source, inverse, side, down = linearise(
                r, place[0] * own + r + shift, total_rows, (lo, hi), t0, None, (conduct, capacity, act, pre), matrix
            )
            ua[r, lo:hi] = (source + dep[r, lo:hi]) * inverse
            cs[r, lo:hi] = side
            cd[r, lo:hi] = down

    return one


def first_rest_kernel(total_rows, scalars, reads, updates, makes, scratch):
    (place,), state, (matrix,) = scalars, reads, scratch
    rows = state[0].shape[0]
    suffix_matrix(matrix)
    over(rest_rows(rows, 1), first_row(total_rows, place, rows - 2 * H, -H, state, updates, matrix))
    sweeps(WIDE, updates, [rest_rows(rows, k) for k in (2, 3, 4)], keeper(state[0], updates[3]))


def later_kernel(outer, last, total_rows, scalars, reads, updates, makes, scratch):
    (place,) = scalars
    lo, hi = NEAR
    if outer:
        above, below, t0, conduct, capacity, act, pre, dep = reads[:8]
        t, ua, cs, cd, ub, uc = updates
        rims = None if last else makes
    else:
        t, t0, conduct, capacity, act, pre, dep = reads
        ua, cs, cd, ub, uc = makes[:5]
        rims = None
    rows = t0.shape[0]
    own = rows - 2 * H
    suffix_matrix(scratch[0])
    if outer:
        t[0:H, lo:hi] = above[...]
        t[H + own :, lo:hi] = below[...]

    def one(r):
        for lo, hi in chunks(NEAR):
            source, inverse, side, down = linearise(
                r, place[0] * own + r - H, total_rows, (lo, hi), t, t0, (conduct, capacity, act, pre), scratch[0]
            )
            ua[r, lo:hi] = (source + dep[r, lo:hi]) * inverse
            cs[r, lo:hi] = side
            cd[r, lo:hi] = down

    if last:
        out, blowing = makes[-2:]
        if outer:
            out[...], blowing[...] = reads[8][...], reads[9][...]
        core = slice(*CORE)

        def finish(r, update):
            value = t[r, core] + update(*CORE)
            out[:, r - H] = value.T.reshape(out.shape[0], 8, LANES)
            p = pre[r, core] * jnp.exp(act[r, core] * value / (1.0 + jnp.abs(value)))
            blowing[pl.ds(r - H, 1), :] = jnp.sum(p.T, axis=0, keepdims=True) * (1.0 / LANES)

    else:
        finish = keeper(t, ub)
    ranges = outer_rows if outer else inner_rows
    over(ranges(rows, 1), one)
    sweeps(NEAR, (ua, cs, cd, ub, uc), [ranges(rows, k) for k in (2, 3, 4)], finish)
    if outer and not last:
        hand_on(ub, rims)


def deliver_kernel(scalars, reads, updates, makes, scratch):
    gathered, arrived = reads
    (out, kelvin), (left, right, sems) = makes, scratch
    copies = [
        pltpu.make_async_copy(arrived.at[s], kelvin.at[:, :, LANES * s : LANES * (s + 1)], sems.at[s])
        for s in range(arrived.shape[0])
    ]
    for copy in copies:
        copy.start()
    groups, rows3, _ = gathered.shape
    rows = rows3 // 3
    me = scalars[0][0]
    owners = gathered[:, 2 * rows :, :].astype(jnp.int32)
    shape = owners.shape
    number = lax.broadcasted_iota(jnp.int32, shape, 0) * rows + lax.broadcasted_iota(jnp.int32, shape, 1)
    first = jnp.min(jnp.where(owners == me, number, groups * rows))
    most = out.shape[0]
    first = jnp.minimum(first, groups * rows - most)
    high_of = lax.broadcasted_iota(jnp.int32, (most, LANES), 0)
    low_of = lax.broadcasted_iota(jnp.int32, (LANES, LANES), 0)
    for i in range(most):
        at = first + i
        group, r = at // rows, at % rows
        value = gathered[group, pl.ds(r, 1), :]
        slot = gathered[group, pl.ds(rows + r, 1), :].astype(jnp.int32)
        owner = gathered[group, pl.ds(2 * rows + r, 1), :].astype(jnp.int32)
        high = jnp.where(owner == me, slot >> 7, -1)
        low = slot & (LANES - 1)
        here = slice(LANES * i, LANES * (i + 1))
        hit = high_of == high
        for k, part in enumerate(split3(value)):
            left[most * k : most * (k + 1), here] = jnp.where(hit, part.astype(jnp.float32), 0.0).astype(
                jnp.bfloat16
            )
        right[:, here] = jnp.where(low_of == low, 1.0, 0.0).astype(jnp.bfloat16)
    parts = lax.dot_general(
        left[...], right[...], (((1,), (1,)), ((), ())), preferred_element_type=jnp.float32
    )
    out[...] = parts[:most] + parts[most : 2 * most] + parts[2 * most :]
    for copy in copies:
        copy.wait()


def shards(
    kelvin_before_step,
    unburnt_resin_share,
    deposited_energy_amount,
    material_label,
    zonal_diffusivity,
    zonal_storage_coefficient,
    frequency_coefficient,
    arrhenius_barrier,
    stream_keeper,
    keeper_position,
):
    own, layers, columns = kelvin_before_step.shape
    n_axial, n_depth = lax.axis_size("axial"), lax.axis_size("depth")
    place = lax.axis_index("axial").astype(jnp.int32).reshape(1)
    total_rows = own * n_axial
    tables = jnp.stack(
        [zonal_diffusivity, zonal_storage_coefficient, frequency_coefficient, arrhenius_barrier]
    )
    rows = own + 2 * H
    extended = (rows, FULL, LANES)
    rim = (H, NEAR[1] - NEAR[0], LANES)
    matrix = [pltpu.VMEM((3 * LANES, LANES), jnp.bfloat16)]

    def up(x):
        return lax.ppermute(x, "axial", [(i, i + 1) for i in range(n_axial - 1)])

    def down(x):
        return lax.ppermute(x, "axial", [(i + 1, i) for i in range(n_axial - 1)])

    cells = [kelvin_before_step, material_label, unburnt_resin_share, deposited_energy_amount]
    cells = [kelvin_before_step, material_label, unburnt_resin_share, deposited_energy_amount]
    cells = [pltpu.with_memory_space_constraint(x, pltpu.HBM) for x in cells]

    def sent(first):
        return call(
            functools.partial(pack_kernel, first), "pack1" if first else "pack2", [], cells, [],
            [(n_depth, len(planes(first, own)), layers, LANES)],
            [pltpu.VMEM(x.shape, x.dtype) for x in cells]
            + [pltpu.VMEM((n_depth, len(planes(first, own)), layers, LANES), jnp.float32)]
            + [pltpu.SemaphoreType.DMA((4, 2)), pltpu.SemaphoreType.DMA((10,))],
            space=pltpu.HBM, out_space=pltpu.HBM,
        )[0]

    arrived = [lax.all_to_all(sent(first), "depth", 0, 0) for first in (True, False)]
    rims = [(n_depth, len(rim_planes(side)), layers, LANES) for side in (1, 0)]
    top, bottom = call(rims_kernel, "rims", [], arrived[:1], [], rims, kept=False)
    own_rims = call(
        unpack_own_kernel, "unpack_own", [tables], arrived[:1], [], [(2 * H, SPAN, LANES)] * 6
    )
    outer = (4 * H, SPAN, LANES)
    came = call(
        functools.partial(outer_kernel, total_rows, own), "newton1_outer",
        [place, tables], [up(top), down(bottom), *own_rims], [], [outer] * 9,
        [pltpu.VMEM((4 * H, FULL, LANES), jnp.float32)] * 9 + matrix + [pltpu.SemaphoreType.DMA((9,))],
        out_space=pltpu.HBM, limit=24,
    )
    came = [pltpu.with_memory_space_constraint(x, pltpu.HBM) for x in [arrived[1], *came]]
    *arrays, top, bottom = call(
        functools.partial(first_kernel, total_rows), "newton1",
        [place, tables], came, [], [extended] * 11 + [rim] * 2,
        matrix
        + [pltpu.VMEM(came[0].shape, jnp.float32)]
        + [pltpu.SemaphoreType.DMA((2,)), pltpu.SemaphoreType.DMA((9, 2))],
        space=pltpu.HBM, limit=8,
    )
    state, work = arrays[:6], arrays[6:]
    work = call(
        functools.partial(first_rest_kernel, total_rows), "newton1_rest", [place], state, work, [], matrix
    )
    t0, conduct, capacity, act, pre, dep = state
    t = work[3]
    for last in (False, True):
        above, below = up(top), down(bottom)
        fixed = [t0, conduct, capacity, act, pre, dep]
        results = [(n_depth, own, layers, LANES), (own, LANES)] if last else []
        work = call(
            functools.partial(later_kernel, False, last, total_rows), "newton3_inner" if last else "newton2_inner",
            [place], [t] + fixed, [], [extended] * 5 + results, matrix,
        )
        work = call(
            functools.partial(later_kernel, True, last, total_rows), "newton3_outer" if last else "newton2_outer",
            [place], [above, below] + fixed + work[5:], [t] + work[:5], results if last else [rim] * 2, matrix,
            kept=not last,
        )
        if not last:
            t, top, bottom = work[4], *work[6:]
    kelvin, blowing = work[6:]

    kelvin = lax.all_to_all(kelvin, "depth", 0, 0)

    faces = jnp.concatenate(
        [blowing, keeper_position.astype(jnp.float32), stream_keeper.astype(jnp.float32)], axis=0
    )
    gathered = lax.all_gather(faces, "axial")
    slots = 2 * own * LANES
    any_space = pl.BlockSpec(memory_space=pl.ANY)
    delivered, kelvin = pl.pallas_call(
        lambda place, *refs: deliver_kernel([place], refs[:2], [], refs[2:4], refs[4:]),
        out_shape=[f32(slots // LANES, LANES), f32(own, layers, columns)],
        in_specs=[SM, VM, any_space],
        out_specs=[VM, any_space],
        scratch_shapes=[
            pltpu.VMEM((3 * slots // LANES, slots), jnp.bfloat16),
            pltpu.VMEM((LANES, slots), jnp.bfloat16),
            pltpu.SemaphoreType.DMA((n_depth,)),
        ],
        compiler_params=pltpu.CompilerParams(vmem_limit_bytes=8 * 1024 * 1024),
        name="deliver",
    )(place, gathered, kelvin)
    return (kelvin, delivered.reshape(slots))


def solution(mesh):
    cells = P("axial", "depth", None)
    faces = P("axial", "depth")
    return jax.shard_map(
        shards,
        mesh=mesh,
        in_specs=(cells, cells, cells, cells, P(), P(), P(), P(), faces, faces),
        out_specs=(cells, P(("axial", "depth"))),
        check_vma=False,
    )
```

```python
import functools

import jax
import jax.numpy as jnp
from jax import lax
from jax.experimental import pallas as pl
from jax.experimental.pallas import tpu as pltpu
from jax.sharding import PartitionSpec as P

SWEEPS = 4
H = 4
W = 12
EDGE = 16
LANES = 128
PAD = 8
SPAN = 2 * EDGE + LANES
FULL = SPAN + 2 * PAD
WIDE = (PAD, PAD + SPAN)
NEAR = (PAD + EDGE // 2, PAD + SPAN - EDGE // 2)
CORE = (PAD + EDGE, PAD + EDGE + LANES)
PACKED = 4 * H * 2 * W // LANES

VM = pl.BlockSpec(memory_space=pltpu.VMEM)
SM = pl.BlockSpec(memory_space=pltpu.SMEM)


def f32(*shape):
    return jax.ShapeDtypeStruct(shape, jnp.float32)


def call(kernel, name, scalars, reads, updates, makes, scratch=(), kept=True, space=pltpu.VMEM, out_space=pltpu.VMEM, limit=8):
    counts = [len(scalars), len(reads), len(updates), len(updates), len(makes), len(scratch)]

    def body(*refs):
        groups, at = [], 0
        for count in counts:
            groups.append(refs[at : at + count])
            at += count
        kernel(groups[0], groups[1], groups[3], groups[4], groups[5])

    first = len(scalars) + len(reads)
    out_spaces = out_space if isinstance(out_space, list) else [out_space] * len(makes)
    results = pl.pallas_call(
        body,
        out_shape=[pltpu.VMEM(u.shape, jnp.float32) for u in updates]
        + [x(s, jnp.float32) if kept else f32(*s) for x, s in zip(out_spaces, makes)],
        in_specs=[SM] * len(scalars)
        + [pl.BlockSpec(memory_space=space)] * len(reads)
        + [VM] * len(updates),
        out_specs=[VM] * len(updates) + [pl.BlockSpec(memory_space=x) for x in out_spaces],
        input_output_aliases={first + i: i for i in range(len(updates))},
        scratch_shapes=list(scratch),
        compiler_params=pltpu.CompilerParams(vmem_limit_bytes=limit * 1024 * 1024),
        name=name,
    )(*scalars, *reads, *updates)
    return list(results)


def lane_iota(rows):
    return lax.broadcasted_iota(jnp.int32, (rows, LANES), 1)


def split3(x):
    a = x.astype(jnp.bfloat16)
    rest = x - a.astype(jnp.float32)
    b = rest.astype(jnp.bfloat16)
    c = (rest - b.astype(jnp.float32)).astype(jnp.bfloat16)
    return a, b, c


def over(ranges, body):
    for low, high in ranges:
        for r in range(low, high):
            body(r)


def groups(first, own):
    return [0, own - H] if first else list(range(H, own - H, H))


def planes(first, own):
    result = []
    for g in groups(first, own):
        result += [(k, g + i) for k in range(4) for i in range(H)]
        result += [(4, (g, j)) for j in range(PACKED)]
    return result


GROUP = 4 * H + PACKED


def rim_planes(side):
    fixed = range(1, H) if side else range(H - 1)
    return list(range(H)) + [k * H + i for k in range(1, 4) for i in fixed] + list(range(4 * H, GROUP))


def pack_kernel(first, scalars, ins, updates, makes, scratch):
    (result,), held, out, sems, out_sems = makes, scratch[:4], scratch[4], scratch[5], scratch[6]
    slices = out.shape[0]
    own = ins[0].shape[0]
    lane = lane_iota(8)
    bands = [slice(0, H), slice(own - H, own)] if first else [slice(H, own - H)]
    copies = {
        (i, j): pltpu.make_async_copy(x.at[band], y.at[band], sems.at[i, j])
        for j, band in enumerate(bands)
        for i, (x, y) in enumerate(zip(ins, held))
    }
    for copy in copies.values():
        copy.start()

    def tile(k, a, s):
        return held[k][a, :, LANES * s : LANES * (s + 1)].astype(jnp.float32)

    sent = []
    order = planes(first, own)
    for p, (kind, a) in enumerate(order):
        if kind < 4:
            band = min(p // GROUP, len(bands) - 1)
            if (kind, band) in copies:
                copies.pop((kind, band)).wait()
            for s in range(slices):
                out[s, p] = tile(kind, a, s)
        else:
            (g, part), place = a, a[1] * LANES
            pieces = range(place // (2 * W), (place + LANES - 1) // (2 * W) + 1)
            turned = {
                m: [pltpu.roll(tile(m % 4, g + m // 4, s), (2 * W * m + W) % LANES, 1) for s in range(slices)]
                for m in pieces
            }
            for s in range(slices):
                value = None
                for m in pieces:
                    for start, piece in (
                        (2 * W * m, turned[m][s - 1]),
                        (2 * W * m + W, turned[m][(s + 1) % slices]),
                    ):
                        value = piece if start <= place else jnp.where(lane >= start - place, piece, value)
                out[s, p] = value
        if (p + 1) % GROUP in (0, 2 * H):
            band = slice(sent[-1][1] if sent else 0, p + 1)
            copy = pltpu.make_async_copy(out.at[:, band], result.at[:, band], out_sems.at[len(sent)])
            copy.start()
            sent.append((copy, p + 1))
    for copy, _ in sent:
        copy.wait()


def rims_kernel(scalars, reads, updates, makes, scratch):
    (arrived,), (top, bottom) = reads, makes
    for side, ref in enumerate((bottom, top)):
        for p, plane in enumerate(rim_planes(side)):
            ref[:, p] = arrived[:, side * GROUP + plane]


def suffix_matrix(m_ref):
    rows, cols = m_ref.shape
    source = lax.broadcasted_iota(jnp.int32, (rows, cols), 0) & (LANES - 1)
    target = lax.broadcasted_iota(jnp.int32, (rows, cols), 1)
    m_ref[...] = jnp.where(source > target, 4.0 / LANES, 0.0).astype(jnp.bfloat16)


def linearise(r, row, total_rows, span, t, t0, fields, m_ref):
    lo, hi = span
    conduct, capacity, act, pre = fields
    lane = lane_iota(hi - lo)
    tc = t[r, lo:hi]
    a = act[r, lo:hi]
    q = 1.0 / (1.0 + jnp.abs(tc))
    aq = a * q
    p = pre[r, lo:hi] * jnp.exp(aq * tc)
    gas = jnp.dot(jnp.concatenate(split3(p), axis=1), m_ref[...], preferred_element_type=jnp.float32)
    c = conduct[r, lo:hi]
    cap = capacity[r, lo:hi]
    deeper = jnp.where(lane == LANES - 1, 0.0, pltpu.roll(tc, LANES - 1, 1))
    shallower = jnp.where(lane == 0, 0.0, pltpu.roll(tc, 1, 1))
    pairs = t[r - 1, lo:hi] + t[r + 1, lo:hi] + t[r, lo - 1 : hi - 1] + t[r, lo + 1 : hi + 1]
    spread = pairs + 2.0 * (deeper + shallower) - 8.0 * tc
    source = c * spread - 0.5 * p - gas * (tc - deeper)
    if t0 is not None:
        source = source - cap * (tc - t0[r, lo:hi])
    diagonal = cap + 8.0 * c + 0.5 * p * (aq * q) + gas
    inside = jnp.where((row >= 0) & (row < total_rows), 1.0, 0.0)
    inverse = inside / diagonal
    return source, inverse, c * inverse, jnp.where(lane == LANES - 1, 0.0, (2.0 * c + gas) * inverse)


CHUNK = 80


def chunks(span):
    lo, hi = span
    return [(c, min(c + CHUNK, hi)) for c in range(lo, hi, CHUNK)]


def sweeps(span, work, ranges, finish):
    first, side, down, b, c = work

    def swept(src, r, lo, hi):
        lane = lane_iota(hi - lo)
        u = src[r, lo:hi]
        pairs = src[r - 1, lo:hi] + src[r + 1, lo:hi] + src[r, lo - 1 : hi - 1] + src[r, lo + 1 : hi + 1]
        shallower = jnp.where(lane == 0, 0.0, pltpu.roll(u, 1, 1))
        deeper = pltpu.roll(u, LANES - 1, 1)
        return first[r, lo:hi] + side[r, lo:hi] * (pairs + 2.0 * shallower) + down[r, lo:hi] * deeper

    def second(r):
        for lo, hi in chunks(span):
            b[r, lo:hi] = swept(first, r, lo, hi)

    def third(r):
        for lo, hi in chunks(span):
            c[r, lo:hi] = swept(b, r, lo, hi)

    def last(r):
        finish(r, lambda lo, hi: swept(c, r, lo, hi))

    over(ranges[0], second)
    over(ranges[1], third)
    over(ranges[2], last)


def inner_rows(rows, k):
    return [(H + k, rows - H - k)]


def outer_rows(rows, k):
    return [(k, H + k), (rows - H - k, rows - k)]


def from_cells(ref, r):
    x = ref[:, r]
    return x.reshape(x.shape[0] * x.shape[1], LANES).T


def unpack_rows(ref, plane_of, first, lo, arrays):
    edges = jnp.concatenate([from_cells(ref, plane_of(4 * H + j)) for j in range(PACKED)], axis=0)
    pad = EDGE - W
    for i in range(H):
        for kind, array in enumerate(arrays):
            plane = plane_of(kind * H + i)
            if plane is None:
                continue
            at = 2 * W * (4 * i + kind)
            array[first + i, lo : lo + EDGE] = pltpu.roll(edges[at : at + EDGE], pad, 0)
            array[first + i, lo + EDGE : lo + EDGE + LANES] = from_cells(ref, plane)
            array[first + i, lo + EDGE + LANES : lo + SPAN] = pltpu.roll(edges[at + 2 * W - EDGE : at + 2 * W], EDGE - pad, 0)


def look_up(tables, r, wide, state):
    _, conduct, capacity, act, pre, _ = state
    label = conduct[r, wide]
    fields = [jnp.full(label.shape, tables[f, 0], jnp.float32) for f in range(4)]
    for zone in range(1, tables.shape[1]):
        here = label == float(zone)
        fields = [jnp.where(here, tables[f, zone], x) for f, x in enumerate(fields)]
    conduct[r, wide] = fields[0]
    capacity[r, wide] = fields[1]
    pre[r, wide] = fields[2] * pre[r, wide]
    act[r, wide] = fields[3]


def keeper(t, t_new):
    def finish(r, update):
        for lo, hi in chunks(NEAR):
            t_new[r, lo:hi] = t[r, lo:hi] + update(lo, hi)

    return finish


def hand_on(t_new, rims):
    own = t_new.shape[0] - 2 * H
    rims[0][...] = t_new[own : own + H, slice(*NEAR)]
    rims[1][...] = t_new[H : 2 * H, slice(*NEAR)]


def unpack_own_kernel(scalars, reads, updates, makes, scratch):
    t0, conduct, capacity, act, pre, dep = makes
    for half in range(2):
        unpack_rows(reads[0], lambda plane: half * GROUP + plane, half * H, 0, (t0, conduct, pre, dep))
    for r in range(2 * H):
        look_up(scalars[0], r, slice(0, SPAN), makes)


def outer_kernel(total_rows, own, scalars, reads, updates, makes, scratch):
    place, tables = scalars
    above, below, own_rims = reads[0], reads[1], reads[2:]
    arrays, matrix, sems = scratch[:9], scratch[9], scratch[10]
    state, work = arrays[:6], arrays[6:]
    t0, conduct, capacity, act, pre, dep = state
    lo, hi = WIDE
    copies = []

    def send(which):
        for i in which:
            copies.append(pltpu.make_async_copy(arrays[i].at[:, lo:hi], makes[i], sems.at[i]))
            copies[-1].start()

    def rim(side):
        table = {plane: p for p, plane in enumerate(rim_planes(side))}
        return table.get

    suffix_matrix(matrix)
    for x, y in zip(own_rims, state):
        y[H : 3 * H, lo:hi] = x[...]
    unpack_rows(above, rim(1), 0, lo, (t0, conduct, pre, dep))
    unpack_rows(below, rim(0), 3 * H, lo, (t0, conduct, pre, dep))
    send([0, 5])
    for r in [*range(1, H), *range(3 * H, 4 * H - 1)]:
        look_up(tables, r, slice(lo, hi), state)
    send([1, 2, 3, 4])
    for first, shift in ((1, -H), (2 * H + 1, own - 3 * H)):
        one = first_row(total_rows, place, own, shift, state, work, matrix)
        over([(first, first + 2 * H - 2)], one)
    send([6, 7, 8])
    for copy in copies:
        copy.wait()


def first_kernel(total_rows, scalars, reads, updates, makes, scratch):
    place, tables = scalars
    arrived, came = reads[0], reads[1:]
    state, work, rims = makes[:6], makes[6:11], makes[11:]
    matrix, held, sem, sems = scratch
    t0, conduct, capacity, act, pre, dep = state
    ua, cs, cd, ub, uc = work
    rows = t0.shape[0]
    own = rows - 2 * H
    lo, hi = WIDE
    firsts = groups(False, own)
    mine = []
    for i in range(len(firsts)):
        band = slice(i * GROUP, (i + 1) * GROUP)
        mine.append(pltpu.make_async_copy(arrived.at[:, band], held.at[:, band], sem.at[i]))
    others = []
    for i, (x, y) in enumerate(zip(came, (*state, ua, cs, cd))):
        edge = 0 if i < 6 else 1
        for half, shift in enumerate((0, own - 2 * H)):
            low, high = half * 2 * H + edge, (half + 1) * 2 * H - edge
            others.append(
                pltpu.make_async_copy(x.at[low:high], y.at[low + shift : high + shift, lo:hi], sems.at[i, half])
            )
    for copy in mine:
        copy.start()
    suffix_matrix(matrix)

    for i, g in enumerate(firsts):
        mine[i].wait()
        if i == 0:
            for copy in others:
                copy.start()
        unpack_rows(held, lambda plane: i * GROUP + plane, g + H, lo, (t0, conduct, pre, dep))
        for r in range(g + H, g + 2 * H):
            look_up(tables, r, slice(lo, hi), state)
    one = first_row(total_rows, place, own, -H, state, work, matrix)
    middle = rows // 2 - 1, rows // 2 + 1
    over([(2 * H + 1, middle[0]), (middle[1], own - 1)], one)
    for copy in others[:12]:
        copy.wait()
    over([(2 * H - 1, 2 * H + 1), (own - 1, own + 1)], one)
    for copy in others[12:]:
        copy.wait()
    sweeps(WIDE, work, [rim_rows(rows, k) for k in (2, 3, 4)], keeper(t0, ub))
    hand_on(ub, rims)


def rim_rows(rows, k):
    return [(k, 3 * H - k), (rows - 3 * H + k, rows - k)]


def rest_rows(rows, k):
    return [(3 * H - k, rows - 3 * H + k)]


def first_row(total_rows, place, own, shift, state, work, matrix):
    t0, conduct, capacity, act, pre, dep = state
    ua, cs, cd = work[:3]

    def one(r):
        for lo, hi in chunks(WIDE):
            source, inverse, side, down = linearise(
                r, place[0] * own + r + shift, total_rows, (lo, hi), t0, None, (conduct, capacity, act, pre), matrix
            )
            ua[r, lo:hi] = (source + dep[r, lo:hi]) * inverse
            cs[r, lo:hi] = side
            cd[r, lo:hi] = down

    return one


def first_rest_kernel(total_rows, scalars, reads, updates, makes, scratch):
    (place,), state, (matrix,) = scalars, reads, scratch
    rows = state[0].shape[0]
    suffix_matrix(matrix)
    over(rest_rows(rows, 1), first_row(total_rows, place, rows - 2 * H, -H, state, updates, matrix))
    sweeps(WIDE, updates, [rest_rows(rows, k) for k in (2, 3, 4)], keeper(state[0], updates[3]))


def later_kernel(outer, last, total_rows, scalars, reads, updates, makes, scratch):
    (place,) = scalars
    lo, hi = NEAR
    if outer:
        above, below, t0, conduct, capacity, act, pre, dep = reads[:8]
        t, ua, cs, cd, ub, uc = updates
        rims = None if last else makes
    else:
        t, t0, conduct, capacity, act, pre, dep = reads
        ua, cs, cd, ub, uc = makes[:5]
        rims = None
    rows = t0.shape[0]
    own = rows - 2 * H
    suffix_matrix(scratch[0])
    if outer:
        t[0:H, lo:hi] = above[...]
        t[H + own :, lo:hi] = below[...]

    def one(r):
        for lo, hi in chunks(NEAR):
            source, inverse, side, down = linearise(
                r, place[0] * own + r - H, total_rows, (lo, hi), t, t0, (conduct, capacity, act, pre), scratch[0]
            )
            ua[r, lo:hi] = (source + dep[r, lo:hi]) * inverse
            cs[r, lo:hi] = side
            cd[r, lo:hi] = down

    if last:
        out, blowing = makes[-2:]
        if outer:
            part, sems = scratch[1:]
            copies = [
                pltpu.make_async_copy(reads[8], out.at[:, H : own - H], sems.at[0]),
                pltpu.make_async_copy(part.at[:, :H], out.at[:, :H], sems.at[1]),
                pltpu.make_async_copy(part.at[:, H:], out.at[:, own - H :], sems.at[2]),
            ]
            copies[0].start()
            blowing[...] = reads[9][...]
        else:
            part = out
        core = slice(*CORE)

        def finish(r, update):
            value = t[r, core] + update(*CORE)
            at = r - 2 * H if not outer else r - H if r < 2 * H else r - own + H
            part[:, at] = value.T.reshape(part.shape[0], 8, LANES)
            p = pre[r, core] * jnp.exp(act[r, core] * value / (1.0 + jnp.abs(value)))
            blowing[pl.ds(r - H, 1), :] = jnp.sum(p.T, axis=0, keepdims=True) * (1.0 / LANES)
            if outer and r in (2 * H - 1, own + H - 1):
                copies[1 if r < own else 2].start()

    else:
        finish = keeper(t, ub)
    ranges = outer_rows if outer else inner_rows
    over(ranges(rows, 1), one)
    sweeps(NEAR, (ua, cs, cd, ub, uc), [ranges(rows, k) for k in (2, 3, 4)], finish)
    if outer and last:
        for copy in copies:
            copy.wait()
    if outer and not last:
        hand_on(ub, rims)


def deliver_kernel(scalars, reads, updates, makes, scratch):
    gathered, arrived = reads
    (out, kelvin), (left, right, sems) = makes, scratch
    copies = [
        pltpu.make_async_copy(arrived.at[s], kelvin.at[:, :, LANES * s : LANES * (s + 1)], sems.at[s])
        for s in range(arrived.shape[0])
    ]
    for copy in copies:
        copy.start()
    groups, rows3, _ = gathered.shape
    rows = rows3 // 3
    me = scalars[0][0]
    owners = gathered[:, 2 * rows :, :].astype(jnp.int32)
    shape = owners.shape
    number = lax.broadcasted_iota(jnp.int32, shape, 0) * rows + lax.broadcasted_iota(jnp.int32, shape, 1)
    first = jnp.min(jnp.where(owners == me, number, groups * rows))
    most = out.shape[0]
    first = jnp.minimum(first, groups * rows - most)
    high_of = lax.broadcasted_iota(jnp.int32, (most, LANES), 0)
    low_of = lax.broadcasted_iota(jnp.int32, (LANES, LANES), 0)

    def one(i, _):
        at = first + i
        group, r = at // rows, at % rows
        value = gathered[group, pl.ds(r, 1), :]
        slot = gathered[group, pl.ds(rows + r, 1), :].astype(jnp.int32)
        owner = gathered[group, pl.ds(2 * rows + r, 1), :].astype(jnp.int32)
        high = jnp.where(owner == me, slot >> 7, -1)
        low = slot & (LANES - 1)
        here = pl.ds(pl.multiple_of(LANES * i, LANES), LANES)
        hit = high_of == high
        for k, part in enumerate(split3(value)):
            left[most * k : most * (k + 1), here] = jnp.where(hit, part.astype(jnp.float32), 0.0).astype(
                jnp.bfloat16
            )
        right[:, here] = jnp.where(low_of == low, 1.0, 0.0).astype(jnp.bfloat16)
        return 0

    lax.fori_loop(0, most, one, 0, unroll=4)
    parts = lax.dot_general(
        left[...], right[...], (((1,), (1,)), ((), ())), preferred_element_type=jnp.float32
    )
    out[...] = parts[:most] + parts[most : 2 * most] + parts[2 * most :]
    for copy in copies:
        copy.wait()


def shards(
    kelvin_before_step,
    unburnt_resin_share,
    deposited_energy_amount,
    material_label,
    zonal_diffusivity,
    zonal_storage_coefficient,
    frequency_coefficient,
    arrhenius_barrier,
    stream_keeper,
    keeper_position,
):
    own, layers, columns = kelvin_before_step.shape
    n_axial, n_depth = lax.axis_size("axial"), lax.axis_size("depth")
    place = lax.axis_index("axial").astype(jnp.int32).reshape(1)
    total_rows = own * n_axial
    tables = jnp.stack(
        [zonal_diffusivity, zonal_storage_coefficient, frequency_coefficient, arrhenius_barrier]
    )
    rows = own + 2 * H
    extended = (rows, FULL, LANES)
    rim = (H, NEAR[1] - NEAR[0], LANES)
    matrix = [pltpu.VMEM((3 * LANES, LANES), jnp.bfloat16)]

    def up(x):
        return lax.ppermute(x, "axial", [(i, i + 1) for i in range(n_axial - 1)])

    def down(x):
        return lax.ppermute(x, "axial", [(i + 1, i) for i in range(n_axial - 1)])

    cells = [kelvin_before_step, material_label, unburnt_resin_share, deposited_energy_amount]
    cells = [kelvin_before_step, material_label, unburnt_resin_share, deposited_energy_amount]
    cells = [pltpu.with_memory_space_constraint(x, pltpu.HBM) for x in cells]

    def sent(first):
        return call(
            functools.partial(pack_kernel, first), "pack1" if first else "pack2", [], cells, [],
            [(n_depth, len(planes(first, own)), layers, LANES)],
            [pltpu.VMEM(x.shape, x.dtype) for x in cells]
            + [pltpu.VMEM((n_depth, len(planes(first, own)), layers, LANES), jnp.float32)]
            + [pltpu.SemaphoreType.DMA((4, 2)), pltpu.SemaphoreType.DMA((10,))],
            space=pltpu.HBM, out_space=pltpu.HBM,
        )[0]

    arrived = [lax.all_to_all(sent(first), "depth", 0, 0) for first in (True, False)]
    rims = [(n_depth, len(rim_planes(side)), layers, LANES) for side in (1, 0)]
    top, bottom = call(rims_kernel, "rims", [], arrived[:1], [], rims, kept=False)
    own_rims = call(
        unpack_own_kernel, "unpack_own", [tables], arrived[:1], [], [(2 * H, SPAN, LANES)] * 6
    )
    outer = (4 * H, SPAN, LANES)
    came = call(
        functools.partial(outer_kernel, total_rows, own), "newton1_outer",
        [place, tables], [up(top), down(bottom), *own_rims], [], [outer] * 9,
        [pltpu.VMEM((4 * H, FULL, LANES), jnp.float32)] * 9 + matrix + [pltpu.SemaphoreType.DMA((9,))],
        out_space=pltpu.HBM, limit=24,
    )
    came = [pltpu.with_memory_space_constraint(x, pltpu.HBM) for x in [arrived[1], *came]]
    *arrays, top, bottom = call(
        functools.partial(first_kernel, total_rows), "newton1",
        [place, tables], came, [], [extended] * 11 + [rim] * 2,
        matrix
        + [pltpu.VMEM(came[0].shape, jnp.float32)]
        + [pltpu.SemaphoreType.DMA((2,)), pltpu.SemaphoreType.DMA((9, 2))],
        space=pltpu.HBM, limit=8,
    )
    state, work = arrays[:6], arrays[6:]
    work = call(
        functools.partial(first_rest_kernel, total_rows), "newton1_rest", [place], state, work, [], matrix
    )
    t0, conduct, capacity, act, pre, dep = state
    t = work[3]
    for last in (False, True):
        above, below = up(top), down(bottom)
        fixed = [t0, conduct, capacity, act, pre, dep]
        part = (n_depth, own - 2 * H, layers, LANES)
        results = [part, (own, LANES)] if last else []
        work = call(
            functools.partial(later_kernel, False, last, total_rows), "newton3_inner" if last else "newton2_inner",
            [place], [t] + fixed, [], [extended] * 5 + results, matrix,
        )
        kwargs = dict(
            makes=[(n_depth, own, layers, LANES), (own, LANES)],
            scratch=matrix
            + [pltpu.VMEM((n_depth, 2 * H, layers, LANES), jnp.float32), pltpu.SemaphoreType.DMA((3,))],
            out_space=[pltpu.HBM, pltpu.VMEM],
        ) if last else dict(makes=[rim] * 2, scratch=matrix)
        work = call(
            functools.partial(later_kernel, True, last, total_rows), "newton3_outer" if last else "newton2_outer",
            [place], [above, below] + fixed + work[5:], [t] + work[:5], **kwargs,
        )
        if not last:
            t, top, bottom = work[4], *work[6:]
    kelvin, blowing = work[6:]

    kelvin = lax.all_to_all(kelvin, "depth", 0, 0)

    faces = jnp.concatenate(
        [blowing, keeper_position.astype(jnp.float32), stream_keeper.astype(jnp.float32)], axis=0
    )
    gathered = lax.all_gather(faces, "axial")
    slots = 2 * own * LANES
    any_space = pl.BlockSpec(memory_space=pl.ANY)
    delivered, kelvin = pl.pallas_call(
        lambda place, *refs: deliver_kernel([place], refs[:2], [], refs[2:4], refs[4:]),
        out_shape=[f32(slots // LANES, LANES), f32(own, layers, columns)],
        in_specs=[SM, VM, any_space],
        out_specs=[VM, any_space],
        scratch_shapes=[
            pltpu.VMEM((3 * slots // LANES, slots), jnp.bfloat16),
            pltpu.VMEM((LANES, slots), jnp.bfloat16),
            pltpu.SemaphoreType.DMA((n_depth,)),
        ],
        compiler_params=pltpu.CompilerParams(vmem_limit_bytes=8 * 1024 * 1024),
        name="deliver",
    )(place, gathered, kelvin)
    return (kelvin, delivered.reshape(slots))


def solution(mesh):
    cells = P("axial", "depth", None)
    faces = P("axial", "depth")
    return jax.shard_map(
        shards,
        mesh=mesh,
        in_specs=(cells, cells, cells, cells, P(), P(), P(), P(), faces, faces),
        out_specs=(cells, P(("axial", "depth"))),
        check_vma=False,
    )
```

```python
import functools

import jax
import jax.numpy as jnp
from jax import lax
from jax.experimental import pallas as pl
from jax.experimental.pallas import tpu as pltpu
from jax.sharding import PartitionSpec as P

SWEEPS = 4
H = 4
W = 12
EDGE = 16
LANES = 128
PAD = 8
SPAN = 2 * EDGE + LANES
FULL = SPAN + 2 * PAD
WIDE = (PAD, PAD + SPAN)
NEAR = (PAD + EDGE // 2, PAD + SPAN - EDGE // 2)
CORE = (PAD + EDGE, PAD + EDGE + LANES)
PACKED = 4 * H * 2 * W // LANES

VM = pl.BlockSpec(memory_space=pltpu.VMEM)
SM = pl.BlockSpec(memory_space=pltpu.SMEM)


def f32(*shape):
    return jax.ShapeDtypeStruct(shape, jnp.float32)


def call(kernel, name, scalars, reads, updates, makes, scratch=(), kept=True, space=pltpu.VMEM, out_space=pltpu.VMEM, limit=8):
    counts = [len(scalars), len(reads), len(updates), len(updates), len(makes), len(scratch)]

    def body(*refs):
        groups, at = [], 0
        for count in counts:
            groups.append(refs[at : at + count])
            at += count
        kernel(groups[0], groups[1], groups[3], groups[4], groups[5])

    first = len(scalars) + len(reads)
    out_spaces = out_space if isinstance(out_space, list) else [out_space] * len(makes)
    results = pl.pallas_call(
        body,
        out_shape=[pltpu.VMEM(u.shape, jnp.float32) for u in updates]
        + [x(s, jnp.float32) if kept else f32(*s) for x, s in zip(out_spaces, makes)],
        in_specs=[SM] * len(scalars)
        + [pl.BlockSpec(memory_space=space)] * len(reads)
        + [VM] * len(updates),
        out_specs=[VM] * len(updates) + [pl.BlockSpec(memory_space=x) for x in out_spaces],
        input_output_aliases={first + i: i for i in range(len(updates))},
        scratch_shapes=list(scratch),
        compiler_params=pltpu.CompilerParams(vmem_limit_bytes=limit * 1024 * 1024),
        name=name,
    )(*scalars, *reads, *updates)
    return list(results)


def lane_iota(rows):
    return lax.broadcasted_iota(jnp.int32, (rows, LANES), 1)


def split3(x):
    a = x.astype(jnp.bfloat16)
    rest = x - a.astype(jnp.float32)
    b = rest.astype(jnp.bfloat16)
    c = (rest - b.astype(jnp.float32)).astype(jnp.bfloat16)
    return a, b, c


def over(ranges, body):
    for low, high in ranges:
        for r in range(low, high):
            body(r)


def groups(first, own):
    return [0, own - H] if first else list(range(H, own - H, H))


def planes(first, own):
    result = []
    for g in groups(first, own):
        result += [(k, g + i) for k in range(4) for i in range(H)]
        result += [(4, (g, j)) for j in range(PACKED)]
    return result


GROUP = 4 * H + PACKED


def rim_planes(side):
    fixed = range(1, H) if side else range(H - 1)
    return list(range(H)) + [k * H + i for k in range(1, 4) for i in fixed] + list(range(4 * H, GROUP))


def pack_kernel(first, scalars, ins, updates, makes, scratch):
    (result,), held, out, sems, out_sems = makes, scratch[:4], scratch[4], scratch[5], scratch[6]
    slices = out.shape[0]
    own = ins[0].shape[0]
    lane = lane_iota(8)
    bands = [slice(0, H), slice(own - H, own)] if first else [slice(H, own - H)]
    copies = {
        (i, j): pltpu.make_async_copy(x.at[band], y.at[band], sems.at[i, j])
        for j, band in enumerate(bands)
        for i, (x, y) in enumerate(zip(ins, held))
    }
    for copy in copies.values():
        copy.start()

    def tile(k, a, s):
        return held[k][a, :, LANES * s : LANES * (s + 1)].astype(jnp.float32)

    sent = []
    order = planes(first, own)
    for p, (kind, a) in enumerate(order):
        if kind < 4:
            band = min(p // GROUP, len(bands) - 1)
            if (kind, band) in copies:
                copies.pop((kind, band)).wait()
            for s in range(slices):
                out[s, p] = tile(kind, a, s)
        else:
            (g, part), place = a, a[1] * LANES
            pieces = range(place // (2 * W), (place + LANES - 1) // (2 * W) + 1)
            turned = {
                m: [pltpu.roll(tile(m % 4, g + m // 4, s), (2 * W * m + W) % LANES, 1) for s in range(slices)]
                for m in pieces
            }
            for s in range(slices):
                value = None
                for m in pieces:
                    for start, piece in (
                        (2 * W * m, turned[m][s - 1]),
                        (2 * W * m + W, turned[m][(s + 1) % slices]),
                    ):
                        value = piece if start <= place else jnp.where(lane >= start - place, piece, value)
                out[s, p] = value
        if (p + 1) % GROUP in (0, 2 * H):
            band = slice(sent[-1][1] if sent else 0, p + 1)
            copy = pltpu.make_async_copy(out.at[:, band], result.at[:, band], out_sems.at[len(sent)])
            copy.start()
            sent.append((copy, p + 1))
    for copy, _ in sent:
        copy.wait()


def rims_kernel(scalars, reads, updates, makes, scratch):
    (arrived,), (top, bottom), (sems,) = reads, makes, scratch
    copies = []
    for side, ref in enumerate((bottom, top)):
        order = rim_planes(side)
        begin = 0
        for p in range(1, len(order) + 1):
            if p < len(order) and order[p] == order[p - 1] + 1:
                continue
            low = side * GROUP + order[begin]
            copies.append(
                pltpu.make_async_copy(
                    arrived.at[:, low : low + p - begin], ref.at[:, begin:p], sems.at[len(copies)]
                )
            )
            copies[-1].start()
            begin = p
    for copy in copies:
        copy.wait()


def suffix_matrix(m_ref):
    rows, cols = m_ref.shape
    source = lax.broadcasted_iota(jnp.int32, (rows, cols), 0) & (LANES - 1)
    target = lax.broadcasted_iota(jnp.int32, (rows, cols), 1)
    m_ref[...] = jnp.where(source > target, 4.0 / LANES, 0.0).astype(jnp.bfloat16)


def linearise(r, row, total_rows, span, t, t0, fields, m_ref):
    lo, hi = span
    conduct, capacity, act, pre = fields
    lane = lane_iota(hi - lo)
    tc = t[r, lo:hi]
    a = act[r, lo:hi]
    q = 1.0 / (1.0 + jnp.abs(tc))
    aq = a * q
    p = pre[r, lo:hi] * jnp.exp(aq * tc)
    gas = jnp.dot(jnp.concatenate(split3(p), axis=1), m_ref[...], preferred_element_type=jnp.float32)
    c = conduct[r, lo:hi]
    cap = capacity[r, lo:hi]
    deeper = jnp.where(lane == LANES - 1, 0.0, pltpu.roll(tc, LANES - 1, 1))
    shallower = jnp.where(lane == 0, 0.0, pltpu.roll(tc, 1, 1))
    pairs = t[r - 1, lo:hi] + t[r + 1, lo:hi] + t[r, lo - 1 : hi - 1] + t[r, lo + 1 : hi + 1]
    spread = pairs + 2.0 * (deeper + shallower) - 8.0 * tc
    source = c * spread - 0.5 * p - gas * (tc - deeper)
    if t0 is not None:
        source = source - cap * (tc - t0[r, lo:hi])
    diagonal = cap + 8.0 * c + 0.5 * p * (aq * q) + gas
    inside = jnp.where((row >= 0) & (row < total_rows), 1.0, 0.0)
    inverse = inside / diagonal
    return source, inverse, c * inverse, jnp.where(lane == LANES - 1, 0.0, (2.0 * c + gas) * inverse)


CHUNK = 80


def chunks(span):
    lo, hi = span
    return [(c, min(c + CHUNK, hi)) for c in range(lo, hi, CHUNK)]


def sweeps(span, work, ranges, finish):
    first, side, down, b, c = work

    def swept(src, r, lo, hi):
        lane = lane_iota(hi - lo)
        u = src[r, lo:hi]
        pairs = src[r - 1, lo:hi] + src[r + 1, lo:hi] + src[r, lo - 1 : hi - 1] + src[r, lo + 1 : hi + 1]
        shallower = jnp.where(lane == 0, 0.0, pltpu.roll(u, 1, 1))
        deeper = pltpu.roll(u, LANES - 1, 1)
        return first[r, lo:hi] + side[r, lo:hi] * (pairs + 2.0 * shallower) + down[r, lo:hi] * deeper

    def second(r):
        for lo, hi in chunks(span):
            b[r, lo:hi] = swept(first, r, lo, hi)

    def third(r):
        for lo, hi in chunks(span):
            c[r, lo:hi] = swept(b, r, lo, hi)

    def last(r):
        finish(r, lambda lo, hi: swept(c, r, lo, hi))

    over(ranges[0], second)
    over(ranges[1], third)
    over(ranges[2], last)


def inner_rows(rows, k):
    return [(H + k, rows - H - k)]


def outer_rows(rows, k):
    return [(k, H + k), (rows - H - k, rows - k)]


def from_cells(ref, r):
    x = ref[:, r]
    return x.reshape(x.shape[0] * x.shape[1], LANES).T


def unpack_rows(ref, plane_of, first, lo, arrays):
    edges = jnp.concatenate([from_cells(ref, plane_of(4 * H + j)) for j in range(PACKED)], axis=0)
    pad = EDGE - W
    for i in range(H):
        for kind, array in enumerate(arrays):
            plane = plane_of(kind * H + i)
            if plane is None:
                continue
            at = 2 * W * (4 * i + kind)
            array[first + i, lo : lo + EDGE] = pltpu.roll(edges[at : at + EDGE], pad, 0)
            array[first + i, lo + EDGE : lo + EDGE + LANES] = from_cells(ref, plane)
            array[first + i, lo + EDGE + LANES : lo + SPAN] = pltpu.roll(edges[at + 2 * W - EDGE : at + 2 * W], EDGE - pad, 0)


def look_up(tables, r, wide, state):
    _, conduct, capacity, act, pre, _ = state
    label = conduct[r, wide]
    fields = [jnp.full(label.shape, tables[f, 0], jnp.float32) for f in range(4)]
    for zone in range(1, tables.shape[1]):
        here = label == float(zone)
        fields = [jnp.where(here, tables[f, zone], x) for f, x in enumerate(fields)]
    conduct[r, wide] = fields[0]
    capacity[r, wide] = fields[1]
    pre[r, wide] = fields[2] * pre[r, wide]
    act[r, wide] = fields[3]


def keeper(t, t_new):
    def finish(r, update):
        for lo, hi in chunks(NEAR):
            t_new[r, lo:hi] = t[r, lo:hi] + update(lo, hi)

    return finish


def hand_on(t_new, rims):
    own = t_new.shape[0] - 2 * H
    rims[0][...] = t_new[own : own + H, slice(*NEAR)]
    rims[1][...] = t_new[H : 2 * H, slice(*NEAR)]


def unpack_own_kernel(scalars, reads, updates, makes, scratch):
    t0, conduct, capacity, act, pre, dep = makes
    for half in range(2):
        unpack_rows(reads[0], lambda plane: half * GROUP + plane, half * H, 0, (t0, conduct, pre, dep))
    for r in range(2 * H):
        look_up(scalars[0], r, slice(0, SPAN), makes)


def outer_kernel(total_rows, own, scalars, reads, updates, makes, scratch):
    place, tables = scalars
    above, below, own_rims = reads[0], reads[1], reads[2:]
    arrays, matrix, sems = scratch[:9], scratch[9], scratch[10]
    state, work = arrays[:6], arrays[6:]
    t0, conduct, capacity, act, pre, dep = state
    lo, hi = WIDE
    copies = []

    def send(which):
        for i in which:
            copies.append(pltpu.make_async_copy(arrays[i].at[:, lo:hi], makes[i], sems.at[i]))
            copies[-1].start()

    def rim(side):
        table = {plane: p for p, plane in enumerate(rim_planes(side))}
        return table.get

    suffix_matrix(matrix)
    for x, y in zip(own_rims, state):
        y[H : 3 * H, lo:hi] = x[...]
    unpack_rows(above, rim(1), 0, lo, (t0, conduct, pre, dep))
    unpack_rows(below, rim(0), 3 * H, lo, (t0, conduct, pre, dep))
    send([0, 5])
    for r in [*range(1, H), *range(3 * H, 4 * H - 1)]:
        look_up(tables, r, slice(lo, hi), state)
    send([1, 2, 3, 4])
    for first, shift in ((1, -H), (2 * H + 1, own - 3 * H)):
        one = first_row(total_rows, place, own, shift, state, work, matrix)
        over([(first, first + 2 * H - 2)], one)
    send([6, 7, 8])
    for copy in copies:
        copy.wait()


def first_kernel(total_rows, scalars, reads, updates, makes, scratch):
    place, tables = scalars
    arrived, came = reads[0], reads[1:]
    state, work, rims = makes[:6], makes[6:11], makes[11:]
    matrix, held, sem, sems = scratch
    t0, conduct, capacity, act, pre, dep = state
    ua, cs, cd, ub, uc = work
    rows = t0.shape[0]
    own = rows - 2 * H
    lo, hi = WIDE
    firsts = groups(False, own)
    mine = []
    for i in range(len(firsts)):
        band = slice(i * GROUP, (i + 1) * GROUP)
        mine.append(pltpu.make_async_copy(arrived.at[:, band], held.at[:, band], sem.at[i]))
    others = []
    for i, (x, y) in enumerate(zip(came, (*state, ua, cs, cd))):
        edge = 0 if i < 6 else 1
        for half, shift in enumerate((0, own - 2 * H)):
            low, high = half * 2 * H + edge, (half + 1) * 2 * H - edge
            others.append(
                pltpu.make_async_copy(x.at[low:high], y.at[low + shift : high + shift, lo:hi], sems.at[i, half])
            )
    for copy in mine:
        copy.start()
    suffix_matrix(matrix)

    for i, g in enumerate(firsts):
        mine[i].wait()
        if i == 0:
            for copy in others:
                copy.start()
        unpack_rows(held, lambda plane: i * GROUP + plane, g + H, lo, (t0, conduct, pre, dep))
        for r in range(g + H, g + 2 * H):
            look_up(tables, r, slice(lo, hi), state)
    one = first_row(total_rows, place, own, -H, state, work, matrix)
    middle = rows // 2 - 1, rows // 2 + 1
    over([(2 * H + 1, middle[0]), (middle[1], own - 1)], one)
    for copy in others[:12]:
        copy.wait()
    over([(2 * H - 1, 2 * H + 1), (own - 1, own + 1)], one)
    for copy in others[12:]:
        copy.wait()
    sweeps(WIDE, work, [rim_rows(rows, k) for k in (2, 3, 4)], keeper(t0, ub))
    hand_on(ub, rims)


def rim_rows(rows, k):
    return [(k, 3 * H - k), (rows - 3 * H + k, rows - k)]


def rest_rows(rows, k):
    return [(3 * H - k, rows - 3 * H + k)]


def first_row(total_rows, place, own, shift, state, work, matrix):
    t0, conduct, capacity, act, pre, dep = state
    ua, cs, cd = work[:3]

    def one(r):
        for lo, hi in chunks(WIDE):
            source, inverse, side, down = linearise(
                r, place[0] * own + r + shift, total_rows, (lo, hi), t0, None, (conduct, capacity, act, pre), matrix
            )
            ua[r, lo:hi] = (source + dep[r, lo:hi]) * inverse
            cs[r, lo:hi] = side
            cd[r, lo:hi] = down

    return one


def first_rest_kernel(total_rows, scalars, reads, updates, makes, scratch):
    (place,), state, (matrix,) = scalars, reads, scratch
    rows = state[0].shape[0]
    suffix_matrix(matrix)
    over(rest_rows(rows, 1), first_row(total_rows, place, rows - 2 * H, -H, state, updates, matrix))
    sweeps(WIDE, updates, [rest_rows(rows, k) for k in (2, 3, 4)], keeper(state[0], updates[3]))


def later_kernel(outer, last, total_rows, scalars, reads, updates, makes, scratch):
    (place,) = scalars
    lo, hi = NEAR
    if outer:
        above, below, t0, conduct, capacity, act, pre, dep = reads[:8]
        t, ua, cs, cd, ub, uc = updates
        rims = None if last else makes
    else:
        t, t0, conduct, capacity, act, pre, dep = reads
        ua, cs, cd, ub, uc = makes[:5]
        rims = None
    rows = t0.shape[0]
    own = rows - 2 * H
    suffix_matrix(scratch[0])
    if outer:
        t[0:H, lo:hi] = above[...]
        t[H + own :, lo:hi] = below[...]

    def one(r):
        for lo, hi in chunks(NEAR):
            source, inverse, side, down = linearise(
                r, place[0] * own + r - H, total_rows, (lo, hi), t, t0, (conduct, capacity, act, pre), scratch[0]
            )
            ua[r, lo:hi] = (source + dep[r, lo:hi]) * inverse
            cs[r, lo:hi] = side
            cd[r, lo:hi] = down

    if last:
        out, blowing = makes[-2:]
        if outer:
            part, sems = scratch[1:]
            copies = [
                pltpu.make_async_copy(reads[8], out.at[:, H : own - H], sems.at[0]),
                pltpu.make_async_copy(part.at[:, :H], out.at[:, :H], sems.at[1]),
                pltpu.make_async_copy(part.at[:, H:], out.at[:, own - H :], sems.at[2]),
            ]
            copies[0].start()
            blowing[...] = reads[9][...]
        else:
            part = out
        core = slice(*CORE)

        def finish(r, update):
            value = t[r, core] + update(*CORE)
            at = r - 2 * H if not outer else r - H if r < 2 * H else r - own + H
            part[:, at] = value.T.reshape(part.shape[0], 8, LANES)
            p = pre[r, core] * jnp.exp(act[r, core] * value / (1.0 + jnp.abs(value)))
            blowing[pl.ds(r - H, 1), :] = jnp.sum(p.T, axis=0, keepdims=True) * (1.0 / LANES)
            if outer and r in (2 * H - 1, own + H - 1):
                copies[1 if r < own else 2].start()

    else:
        finish = keeper(t, ub)
    ranges = outer_rows if outer else inner_rows
    over(ranges(rows, 1), one)
    sweeps(NEAR, (ua, cs, cd, ub, uc), [ranges(rows, k) for k in (2, 3, 4)], finish)
    if outer and last:
        for copy in copies:
            copy.wait()
    if outer and not last:
        hand_on(ub, rims)


def deliver_kernel(scalars, reads, updates, makes, scratch):
    gathered, arrived = reads
    (out, kelvin), (left, right, sems) = makes, scratch
    copies = [
        pltpu.make_async_copy(arrived.at[s], kelvin.at[:, :, LANES * s : LANES * (s + 1)], sems.at[s])
        for s in range(arrived.shape[0])
    ]
    for copy in copies:
        copy.start()
    groups, rows3, _ = gathered.shape
    rows = rows3 // 3
    me = scalars[0][0]
    owners = gathered[:, 2 * rows :, :].astype(jnp.int32)
    shape = owners.shape
    number = lax.broadcasted_iota(jnp.int32, shape, 0) * rows + lax.broadcasted_iota(jnp.int32, shape, 1)
    first = jnp.min(jnp.where(owners == me, number, groups * rows))
    most = out.shape[0]
    first = jnp.minimum(first, groups * rows - most)
    high_of = lax.broadcasted_iota(jnp.int32, (most, LANES), 0)
    low_of = lax.broadcasted_iota(jnp.int32, (LANES, LANES), 0)

    def one(i, _):
        at = first + i
        group, r = at // rows, at % rows
        value = gathered[group, pl.ds(r, 1), :]
        slot = gathered[group, pl.ds(rows + r, 1), :].astype(jnp.int32)
        owner = gathered[group, pl.ds(2 * rows + r, 1), :].astype(jnp.int32)
        high = jnp.where(owner == me, slot >> 7, -1)
        low = slot & (LANES - 1)
        here = pl.ds(pl.multiple_of(LANES * i, LANES), LANES)
        hit = high_of == high
        for k, part in enumerate(split3(value)):
            left[most * k : most * (k + 1), here] = jnp.where(hit, part.astype(jnp.float32), 0.0).astype(
                jnp.bfloat16
            )
        right[:, here] = jnp.where(low_of == low, 1.0, 0.0).astype(jnp.bfloat16)
        return 0

    lax.fori_loop(0, most, one, 0, unroll=4)
    parts = lax.dot_general(
        left[...], right[...], (((1,), (1,)), ((), ())), preferred_element_type=jnp.float32
    )
    out[...] = parts[:most] + parts[most : 2 * most] + parts[2 * most :]
    for copy in copies:
        copy.wait()


def shards(
    kelvin_before_step,
    unburnt_resin_share,
    deposited_energy_amount,
    material_label,
    zonal_diffusivity,
    zonal_storage_coefficient,
    frequency_coefficient,
    arrhenius_barrier,
    stream_keeper,
    keeper_position,
):
    own, layers, columns = kelvin_before_step.shape
    n_axial, n_depth = lax.axis_size("axial"), lax.axis_size("depth")
    place = lax.axis_index("axial").astype(jnp.int32).reshape(1)
    total_rows = own * n_axial
    tables = jnp.stack(
        [zonal_diffusivity, zonal_storage_coefficient, frequency_coefficient, arrhenius_barrier]
    )
    rows = own + 2 * H
    extended = (rows, FULL, LANES)
    rim = (H, NEAR[1] - NEAR[0], LANES)
    matrix = [pltpu.VMEM((3 * LANES, LANES), jnp.bfloat16)]

    def up(x):
        return lax.ppermute(x, "axial", [(i, i + 1) for i in range(n_axial - 1)])

    def down(x):
        return lax.ppermute(x, "axial", [(i + 1, i) for i in range(n_axial - 1)])

    cells = [kelvin_before_step, material_label, unburnt_resin_share, deposited_energy_amount]
    cells = [kelvin_before_step, material_label, unburnt_resin_share, deposited_energy_amount]
    cells = [pltpu.with_memory_space_constraint(x, pltpu.HBM) for x in cells]

    def sent(first):
        return call(
            functools.partial(pack_kernel, first), "pack1" if first else "pack2", [], cells, [],
            [(n_depth, len(planes(first, own)), layers, LANES)],
            [pltpu.VMEM(x.shape, x.dtype) for x in cells]
            + [pltpu.VMEM((n_depth, len(planes(first, own)), layers, LANES), jnp.float32)]
            + [pltpu.SemaphoreType.DMA((4, 2)), pltpu.SemaphoreType.DMA((10,))],
            space=pltpu.HBM, out_space=pltpu.HBM,
        )[0]

    arrived = [lax.all_to_all(sent(first), "depth", 0, 0) for first in (True, False)]
    rims = [(n_depth, len(rim_planes(side)), layers, LANES) for side in (1, 0)]
    top, bottom = call(
        rims_kernel, "rims", [], arrived[:1], [], rims, [pltpu.SemaphoreType.DMA((10,))],
        space=pl.ANY, out_space=pltpu.HBM,
    )
    own_rims = call(
        unpack_own_kernel, "unpack_own", [tables], arrived[:1], [], [(2 * H, SPAN, LANES)] * 6
    )
    outer = (4 * H, SPAN, LANES)
    came = call(
        functools.partial(outer_kernel, total_rows, own), "newton1_outer",
        [place, tables], [up(top), down(bottom), *own_rims], [], [outer] * 9,
        [pltpu.VMEM((4 * H, FULL, LANES), jnp.float32)] * 9 + matrix + [pltpu.SemaphoreType.DMA((9,))],
        out_space=pltpu.HBM, limit=24,
    )
    came = [pltpu.with_memory_space_constraint(x, pltpu.HBM) for x in [arrived[1], *came]]
    *arrays, top, bottom = call(
        functools.partial(first_kernel, total_rows), "newton1",
        [place, tables], came, [], [extended] * 11 + [rim] * 2,
        matrix
        + [pltpu.VMEM(came[0].shape, jnp.float32)]
        + [pltpu.SemaphoreType.DMA((2,)), pltpu.SemaphoreType.DMA((9, 2))],
        space=pltpu.HBM, limit=8,
    )
    state, work = arrays[:6], arrays[6:]
    work = call(
        functools.partial(first_rest_kernel, total_rows), "newton1_rest", [place], state, work, [], matrix
    )
    t0, conduct, capacity, act, pre, dep = state
    t = work[3]
    for last in (False, True):
        above, below = up(top), down(bottom)
        fixed = [t0, conduct, capacity, act, pre, dep]
        part = (n_depth, own - 2 * H, layers, LANES)
        results = [part, (own, LANES)] if last else []
        work = call(
            functools.partial(later_kernel, False, last, total_rows), "newton3_inner" if last else "newton2_inner",
            [place], [t] + fixed, [], [extended] * 5 + results, matrix,
        )
        kwargs = dict(
            makes=[(n_depth, own, layers, LANES), (own, LANES)],
            scratch=matrix
            + [pltpu.VMEM((n_depth, 2 * H, layers, LANES), jnp.float32), pltpu.SemaphoreType.DMA((3,))],
            out_space=[pltpu.HBM, pltpu.VMEM],
        ) if last else dict(makes=[rim] * 2, scratch=matrix)
        work = call(
            functools.partial(later_kernel, True, last, total_rows), "newton3_outer" if last else "newton2_outer",
            [place], [above, below] + fixed + work[5:], [t] + work[:5], **kwargs,
        )
        if not last:
            t, top, bottom = work[4], *work[6:]
    kelvin, blowing = work[6:]

    kelvin = lax.all_to_all(kelvin, "depth", 0, 0)

    faces = jnp.concatenate(
        [blowing, keeper_position.astype(jnp.float32), stream_keeper.astype(jnp.float32)], axis=0
    )
    gathered = lax.all_gather(faces, "axial")
    slots = 2 * own * LANES
    any_space = pl.BlockSpec(memory_space=pl.ANY)
    delivered, kelvin = pl.pallas_call(
        lambda place, *refs: deliver_kernel([place], refs[:2], [], refs[2:4], refs[4:]),
        out_shape=[f32(slots // LANES, LANES), f32(own, layers, columns)],
        in_specs=[SM, VM, any_space],
        out_specs=[VM, any_space],
        scratch_shapes=[
            pltpu.VMEM((3 * slots // LANES, slots), jnp.bfloat16),
            pltpu.VMEM((LANES, slots), jnp.bfloat16),
            pltpu.SemaphoreType.DMA((n_depth,)),
        ],
        compiler_params=pltpu.CompilerParams(vmem_limit_bytes=8 * 1024 * 1024),
        name="deliver",
    )(place, gathered, kelvin)
    return (kelvin, delivered.reshape(slots))


def solution(mesh):
    cells = P("axial", "depth", None)
    faces = P("axial", "depth")
    return jax.shard_map(
        shards,
        mesh=mesh,
        in_specs=(cells, cells, cells, cells, P(), P(), P(), P(), faces, faces),
        out_specs=(cells, P(("axial", "depth"))),
        check_vma=False,
    )
```
